32 devices in a mesh: dp: 8 (over y, x, core), seq: 4 (over z).
Axes of the slice: x: 2, y: 2, z: 4, core: 2. Of those that a mesh axis runs over, the one named last changes fastest.
Arguments:
- tokens: bfloat16 [16, 1024, 1024], P('dp', 'seq'), may hold values from -17 to 17
- positions: int32 [16, 1024], P('dp', 'seq'), may hold values from 0 to 4092, as said below
- cotangent: bfloat16 [16, 1024, 1024], P('dp', 'seq'), may hold values from -6 to 6
- q_weight: bfloat16 [1024, 1024], P('dp'), may hold values from -0.1875 to 0.1875
- key_matrix: bfloat16 [1024, 512], P('dp'), may hold values from -0.1875 to 0.1875
- value_matrix: bfloat16 [1024, 512], P('dp'), may hold values from -0.1875 to 0.1875
- out_weight: bfloat16 [1024, 1024], P('dp'), may hold values from -2 to 2
- gate_weight: bfloat16 [1024, 4608], P('dp'), may hold values from -0.1875 to 0.1875
- up_weight: bfloat16 [1024, 4608], P('dp'), may hold values from -0.1875 to 0.1875
- down_weight: bfloat16 [1024, 4608], P('dp'), may hold values from -0.375 to 0.375
- attn_gain: float32 [1024], replicated, may hold values from 0.1 to 1.9
- ffn_gain: float32 [1024], replicated, may hold values from 0.1 to 1.9
- q_gain: float32 [64], replicated, may hold values from 0.1 to 1.9
- k_gain: float32 [64], replicated, may hold values from 0.1 to 1.9
Outputs:
- output: bfloat16 [16, 1024, 1024], P('dp', 'seq')
- input_grad: bfloat16 [16, 1024, 1024], P('dp', 'seq')
- q_weight_grad: float32 [1024, 1024], P('dp')
- k_weight_grad: float32 [1024, 512], P('dp')
- v_weight_grad: float32 [1024, 512], P('dp')
- out_weight_grad: float32 [1024, 1024], P('dp')
- gate_weight_grad: float32 [1024, 4608], P('dp')
- up_weight_grad: float32 [1024, 4608], P('dp')
- down_weight_grad: float32 [1024, 4608], P('dp')
- attn_gain_grad: float32 [1024], replicated
- ffn_gain_grad: float32 [1024], replicated
- q_gain_grad: float32 [64], replicated
- k_gain_grad: float32 [64], replicated
The draws below stay inside these ranges and needn't reach their ends.
Inputs may be any that keep to these rules, and one draw needn't show every extreme that they name: Along each sequence the positions rise by 1 to 4 from one token to the next, the first being 0; in one sequence every step is 4.
All inputs are finite; a program needn't handle non-finite values.
Results may differ from the reference program's by a relative error of at most 0.02.
Values may be sent and summed in bfloat16 or wider, within the bound.
No kernel may reach another device: no remote copies, remote signals or barrier semaphores. Data moves between devices by JAX's collectives and lax.ppermute only.
A program may use at most 320 MiB of HBM per device.

```python
import jax
import jax.numpy as jnp
from jax import lax

MODEL_FEATURES = 1024
QUERY_HEADS = 16
KEY_VALUE_HEADS = 8
HEAD_SIZE = 64
FF = 4608
BATCH = 16
LENGTH = 1024


def draw_tokens(key, part):
    base_key, row_key, col_key = jax.random.split(key, 3)
    shape_all = (BATCH, LENGTH, MODEL_FEATURES)
    row_factor = jnp.exp(jax.random.uniform(row_key, (BATCH, LENGTH, 1), jnp.float32, -1.6, 0.7))
    col_factor = jnp.exp(jax.random.uniform(col_key, (1, 1, MODEL_FEATURES), jnp.float32, -1.6, 0.7))
    base_draw = jax.random.truncated_normal(base_key, -4.0, 4.0, shape_all, jnp.float32)
    return (base_draw * row_factor * col_factor).astype(jnp.bfloat16)


def draw_positions(key, part):
    step_key = jax.random.fold_in(key, 11)
    pick_key = jax.random.fold_in(key, 23)
    position_steps = jax.random.randint(step_key, (BATCH, LENGTH), 1, 5)
    chosen = jax.random.randint(pick_key, (), 0, BATCH)
    full_stride = jnp.arange(BATCH, dtype=jnp.int32)[:, None] == chosen
    position_steps = jnp.where(full_stride, 4, position_steps)
    return (jnp.cumsum(position_steps, axis=1) - position_steps).astype(jnp.int32)


def spiked(values, rng, source, target, shards_of, factor):
    owner, partner = [(jnp.arange(values.shape[axis_at]) // (values.shape[axis_at] // shards_of)).reshape([-1 if axis == axis_at else 1 for axis in range(values.ndim)]) for axis_at in (source, target)]
    chosen = jax.random.permutation(rng, shards_of)[partner]
    strong = (owner == chosen) | (owner == (partner + shards_of // 2) % shards_of)
    return jnp.where(strong, factor * values, values)


def levels(key, dims, cuts, smallest, high):
    factor_of, own = 1.0, jax.random.fold_in(key, 6)
    for dim, parts in cuts:
        heights = jnp.exp(jax.random.uniform(jax.random.fold_in(own, dim), (parts,), jnp.float32, smallest / len(cuts), high / len(cuts)))
        factor_of = factor_of * jnp.repeat(heights, dims[dim] // parts).reshape([-1 if axis == dim else 1 for axis in range(len(dims))])
    return factor_of


def centred(stream_key, dims, width, reach, cuts=(), kind=jnp.bfloat16):
    drawn = width * jax.random.normal(stream_key, dims, jnp.float32)
    if cuts:
        drawn = drawn * levels(stream_key, dims, cuts, -0.22, 0.18)
    return jnp.clip(drawn, -reach, reach).astype(kind)


def bell_draw_with(own_key, extent, spread, bound, cuts, heavy, kind=jnp.bfloat16):
    entries = spread * jax.random.normal(own_key, extent, jnp.float32)
    if cuts:
        entries = entries * levels(own_key, extent, cuts, -0.22, 0.18)
    return jnp.clip(spiked(entries, jax.random.fold_in(own_key, 3), *heavy), -bound, bound).astype(kind)


def setup_inputs(seed: int = 0) -> dict:
    streams_of = jax.random.split(jax.random.key(seed), 15)
    return {
        "tokens": draw_tokens(jax.random.fold_in(streams_of[14], 71), 0),
        "positions": draw_positions(jax.random.fold_in(streams_of[14], 71), 0),
        "cotangent": bell_draw_with(streams_of[2], (BATCH, LENGTH, MODEL_FEATURES), 1.0, 6.0, ((0, 8), (1, 4)), (0, 2, 8, 2.0)),
        "q_weight": centred(streams_of[3], (MODEL_FEATURES, QUERY_HEADS * HEAD_SIZE), MODEL_FEATURES ** -0.5, 0.1875, ((0, 8),)),
        "key_matrix": centred(streams_of[4], (MODEL_FEATURES, KEY_VALUE_HEADS * HEAD_SIZE), MODEL_FEATURES ** -0.5, 0.1875, ((0, 8),)),
        "value_matrix": centred(streams_of[5], (MODEL_FEATURES, KEY_VALUE_HEADS * HEAD_SIZE), MODEL_FEATURES ** -0.5, 0.1875, ((0, 8),)),
        "out_weight": centred(streams_of[6], (MODEL_FEATURES, QUERY_HEADS * HEAD_SIZE), (QUERY_HEADS * HEAD_SIZE // 128) ** -0.5, 2.0, ((0, 8),)),
        "gate_weight": centred(streams_of[7], (MODEL_FEATURES, FF), MODEL_FEATURES ** -0.5, 0.1875, ((0, 8),)),
        "up_weight": centred(streams_of[8], (MODEL_FEATURES, FF), MODEL_FEATURES ** -0.5, 0.1875, ((0, 8),)),
        "down_weight": centred(streams_of[9], (MODEL_FEATURES, FF), (FF // 16) ** -0.5, 0.375, ((0, 8),)),
        "attn_gain": jnp.clip(1.0 + 0.18 * jax.random.normal(streams_of[10], (MODEL_FEATURES,), jnp.float32), 0.1, 1.9),
        "ffn_gain": jnp.clip(1.0 + 0.18 * jax.random.normal(streams_of[11], (MODEL_FEATURES,), jnp.float32), 0.1, 1.9),
        "q_gain": jnp.clip(1.0 + 0.18 * jax.random.normal(streams_of[12], (HEAD_SIZE,), jnp.float32), 0.1, 1.9),
        "k_gain": jnp.clip(1.0 + 0.18 * jax.random.normal(streams_of[13], (HEAD_SIZE,), jnp.float32), 0.1, 1.9),
    }


epsilon = 1e-05
rope_base = 1000000.0
highest_precision = lax.Precision.HIGHEST

@jax.custom_vjp
def low(v):
    return lax.optimization_barrier(v.astype(jnp.bfloat16)).astype(jnp.float32)

@jax.custom_vjp
def low_back(v):
    return v

def low_keep(v):
    return (low(v), None)

def low_pass(kept, grad):
    return (grad,)

def back_keep(v):
    return (v, None)

def back_low(kept, grad):
    return (low(grad),)
low.defvjp(low_keep, low_pass)
low_back.defvjp(back_keep, back_low)

def rms_scale(value_heads):
    return lax.rsqrt(lax.optimization_barrier(jnp.mean(value_heads * value_heads, axis=-1, keepdims=True)) + epsilon)

def rotate(value_heads, cosines, sine_table):
    half_dim = value_heads.shape[-1] // 2
    first_half = value_heads[..., :half_dim]
    second_half = value_heads[..., half_dim:]
    return jnp.concatenate([first_half * cosines - second_half * sine_table, second_half * cosines + first_half * sine_table], axis=-1)

def angles(positions, head_dim):
    freq_index = jnp.arange(head_dim // 2, dtype=jnp.float32)
    inverse = rope_base ** (-(2.0 * freq_index) / head_dim)
    turned = positions.astype(jnp.float32)[:, None] * inverse[None, :]
    return (jnp.cos(turned)[:, None, :], jnp.sin(turned)[:, None, :])

def sequence_forward(tokens_f, positions, q_weight, key_matrix, value_matrix, out_weight, gate_weight, up_weight, down_weight, attn_gain, ffn_gain, q_gain, k_gain):
    sequence_length = tokens_f.shape[0]
    normed_in = low(tokens_f * rms_scale(tokens_f) * attn_gain)
    q_proj = low_back(jnp.dot(normed_in, q_weight, precision=highest_precision))
    key_projected = low_back(jnp.dot(normed_in, key_matrix, precision=highest_precision))
    value_heads = low(low_back(jnp.dot(normed_in, value_matrix, precision=highest_precision)))
    cosines, sine_table = angles(positions, HEAD_SIZE)
    q_heads = q_proj.reshape(sequence_length, QUERY_HEADS, HEAD_SIZE)
    query_rows_all = low(low_back(rotate(q_heads * rms_scale(q_heads) * q_gain, cosines, sine_table)))
    key_heads = key_projected.reshape(sequence_length, KEY_VALUE_HEADS, HEAD_SIZE)
    key_rows = low(low_back(rotate(key_heads * rms_scale(key_heads) * k_gain, cosines, sine_table)))
    grouped_queries = query_rows_all.reshape(sequence_length, KEY_VALUE_HEADS, QUERY_HEADS // KEY_VALUE_HEADS, HEAD_SIZE)
    scores = jnp.einsum('qhgd,khd->hgqk', grouped_queries, key_rows, precision=highest_precision) * HEAD_SIZE ** (-0.5)
    scores = low_back(scores)
    allowed = positions[None, :] <= positions[:, None]
    scores = jnp.where(allowed, scores, -1e+30)
    attention_probs = low(jax.nn.softmax(scores, axis=-1))
    attended_output = jnp.einsum('xiyn,nxo->yxio', attention_probs, value_heads.reshape(sequence_length, KEY_VALUE_HEADS, HEAD_SIZE), precision=highest_precision)
    mixed_heads = low(low_back(attended_output.reshape(sequence_length, QUERY_HEADS * HEAD_SIZE)))
    attn_branch = low_back(jnp.dot(mixed_heads, out_weight.T, precision=highest_precision))
    residual = tokens_f + attn_branch
    normed_mid = low(residual * rms_scale(residual) * ffn_gain)
    gate_proj = low_back(jnp.dot(normed_mid, gate_weight, precision=highest_precision))
    up_proj = low_back(jnp.dot(normed_mid, up_weight, precision=highest_precision))
    hidden = low(jax.nn.silu(gate_proj) * up_proj)
    ffn_branch = low_back(jnp.dot(hidden, down_weight.T, precision=highest_precision))
    return residual + ffn_branch

def reference(tokens, positions, cotangent, q_weight, key_matrix, value_matrix, out_weight, gate_weight, up_weight, down_weight, attn_gain, ffn_gain, q_gain, k_gain):
    params = tuple((weight_arg.astype(jnp.float32) for weight_arg in (q_weight, key_matrix, value_matrix, out_weight, gate_weight, up_weight, down_weight, attn_gain, ffn_gain, q_gain, k_gain)))

    def one_sequence(totals, inputs):
        seq_tokens, seq_positions, seq_cot = inputs

        def forward(tokens_f, *weights_f):
            return sequence_forward(tokens_f, seq_positions, *weights_f)
        result, pullback = jax.vjp(forward, seq_tokens.astype(jnp.float32), *params)
        grads = pullback(seq_cot.astype(jnp.float32))
        new_totals = tuple((held + fresh for held, fresh in zip(totals, grads[1:])))
        return (new_totals, (result.astype(jnp.bfloat16), grads[0].astype(jnp.bfloat16)))
    initial = tuple((jnp.zeros_like(param_arr) for param_arr in params))
    totals, outs_pair = lax.scan(one_sequence, initial, (tokens, positions, cotangent))
    return (outs_pair[0], outs_pair[1], totals[0], totals[1], totals[2], totals[3], totals[4], totals[5], totals[6], totals[7], totals[8], totals[9], totals[10])
```

```python
import functools

import jax
import jax.numpy as jnp
from jax import lax
from jax.experimental import pallas as pl
from jax.experimental.pallas import tpu as pltpu
from jax.sharding import Mesh, PartitionSpec as P

epsilon = 1e-05
rope_base = 1000000.0
f32 = jnp.float32
bf16 = jnp.bfloat16
SWAP = ((0, 1), (1, 0))
EVERY = ("o", "x", "c", "z", "s")
NT = (((1,), (1,)), ((), ()))
NN = (((1,), (0,)), ((), ()))


def dot(left, right, dims=NN):
    return lax.dot_general(left, right, dims, preferred_element_type=f32)


def rms_scale(rows):
    return lax.rsqrt(jnp.mean(rows * rows, axis=-1, keepdims=True) + epsilon)


def norm_back(grad_out, normed_hat, inv_scale, gain):
    scaled = grad_out * gain
    return inv_scale * (scaled - normed_hat * jnp.mean(scaled * normed_hat, axis=-1, keepdims=True))


def square():
    return lax.axis_size("o") == 2 and lax.axis_size("x") == 2


def pair_group():
    return lax.axis_size("s") == 1


def relative(array):
    if not square():
        return array
    quarter = array.shape[-1] // 4
    blocks = [array[..., i * quarter : (i + 1) * quarter] for i in range(4)]
    here_x = lax.axis_index("x") == 1
    here_o = lax.axis_index("o") == 1
    blocks = [jnp.where(here_x, blocks[i ^ 1], blocks[i]) for i in range(4)]
    blocks = [jnp.where(here_o, blocks[i ^ 2], blocks[i]) for i in range(4)]
    return jnp.concatenate(blocks, axis=-1)


def by_core(own, other, axis):
    first = lax.axis_index("c") == 0
    return jnp.concatenate([jnp.where(first, own, other), jnp.where(first, other, own)], axis=axis)


def swap_core(array):
    return lax.ppermute(array, "c", SWAP)


def half_of(array, axis, which):
    size = array.shape[axis] // 2
    low = lax.slice_in_dim(array, 0, size, axis=axis)
    high = lax.slice_in_dim(array, size, 2 * size, axis=axis)
    return jnp.where(which == 0, low, high)


def group_gather(rows):
    if pair_group():
        return by_core(rows[None], swap_core(rows)[None], 0)
    return lax.all_gather(rows, ("s", "c"), axis=0)


def group_scatter(parts):
    if pair_group():
        core = lax.axis_index("c")
        away = sum(half_of(p, 0, 1 - core)[0].astype(f32) for p in parts).astype(bf16)
        mine = sum(half_of(p, 0, core)[0].astype(f32) for p in parts)
        return mine + swap_core(away).astype(f32)
    total = sum(p.astype(f32) for p in parts)
    return lax.psum_scatter(total, ("s", "c"), scatter_dimension=0, tiled=False)


def to_sequence(rows):
    core = lax.axis_index("c")
    away = half_of(rows, 1, 1 - core)
    mine = half_of(rows, 1, core)
    every = by_core(mine, swap_core(away), 0)
    return lax.all_to_all(every, "z", 0, 0, tiled=True)


def from_sequence(rows):
    core = lax.axis_index("c")
    every = lax.all_to_all(rows, "z", 0, 0, tiled=True)
    away = half_of(every, 0, 1 - core)
    mine = half_of(every, 0, core)
    return by_core(mine, swap_core(away), 1)


def gather_rows(parts):
    core = lax.axis_index("c")
    low, high = parts
    mine = jnp.where(core == 0, low, high)
    away = jnp.where(core == 0, high, low)
    own = by_core(mine, swap_core(away), 1)
    if square():
        half = own.shape[1] // 2
        by_x = lax.ppermute(own, "x", SWAP)
        by_o = lax.ppermute(own, "o", SWAP)
        diag_low = lax.ppermute(by_x[:, :half], "o", SWAP)
        diag_high = lax.ppermute(by_o[:, half:], "x", SWAP)
        return [own, by_x, by_o, diag_low, diag_high]
    return [lax.all_gather(own, ("o", "x"), axis=1, tiled=True)]


def grad_slots(model):
    if square():
        return [(2, 0), (3, 0), (0, 0), (3, 1), (2, 1), (1, 0), (0, 1), (1, 1)], [2, 2, 2, 2]
    return [(0, i) for i in range(8)], [8]


def line_sum(part):
    if lax.axis_size("z") != 4:
        return lax.psum(part.astype(f32), "z")
    at = lax.axis_index("z")
    total = part + lax.ppermute(part, "z", ((0, 1), (3, 2))).astype(f32)
    total = total.astype(bf16)
    total = (total.astype(f32) + lax.ppermute(total, "z", ((1, 2), (2, 1))).astype(f32)).astype(bf16)
    back = lax.ppermute(total, "z", ((1, 0), (2, 3)))
    return jnp.where((at == 0) | (at == 3), back, total)


def reduce_rows(outs):
    if square():
        send_a, send_b, keep_a, keep_b = outs
        half = keep_a.shape[1] // 2
        come_a = lax.ppermute(send_a, "x", SWAP)
        come_b = lax.ppermute(send_b, "o", SWAP)

        def add(left, right, which):
            span = slice(which * half, (which + 1) * half)
            return left[:, span].astype(f32) + right[:, span].astype(f32)

        last_a = lax.ppermute(add(keep_a, come_a, 1).astype(bf16), "o", SWAP)
        last_b = lax.ppermute(add(keep_b, come_b, 1).astype(bf16), "x", SWAP)
        low = (add(keep_a, come_a, 0) + last_a.astype(f32)).astype(bf16)
        high = (add(keep_b, come_b, 0) + last_b.astype(f32)).astype(bf16)
    else:
        full = lax.psum_scatter(outs[0].astype(f32), ("o", "x"), scatter_dimension=1, tiled=True)
        half = full.shape[1] // 2
        low, high = full[:, :half].astype(bf16), full[:, half:].astype(bf16)
    low, high = line_sum(low), line_sum(high)
    core = lax.axis_index("c")
    mine = jnp.where(core == 0, low, high)
    away = jnp.where(core == 0, high, low)
    if pair_group():
        other = swap_core(away)
        return [jnp.where(core == 0, mine, other), jnp.where(core == 0, other, mine)]
    both = by_core(mine[None], swap_core(away)[None], 0)
    every = lax.all_gather(both, "s", axis=0, tiled=True)
    return [every[i] for i in range(every.shape[0])]


def fill(scratch, refs, take):
    row = 0
    for ref in refs:
        block = take(ref)
        scratch[row : row + block.shape[0], :] = block
        row += block.shape[0]


def ffn_kernel(blocks, slots, steps, x_ref, xt_ref, cot_ref, cott_ref, *rest):
    weights, rest = rest[:blocks], rest[blocks:]
    outs = max(o for o, _ in slots) + 1
    out_ref, mid_ref = rest[0], rest[1]
    grads = rest[2 : 2 + outs]
    gate, up, down, hid, dgate, dup, out_acc, mid_acc = rest[2 + outs :]
    step = pl.program_id(0)
    for i, scratch in enumerate((gate, up, down)):
        fill(scratch, weights, lambda ref: ref[i])

    @pl.when(step == 0)
    def _():
        out_acc[...] = jnp.zeros_like(out_acc)
        mid_acc[...] = jnp.zeros_like(mid_acc)

    rows = 256

    def body(i, carry):
        at = pl.ds(pl.multiple_of(i * rows, rows), rows)
        x = x_ref[at, :]
        g = dot(x, gate[...])
        u = dot(x, up[...])
        dh = dot(cot_ref[at, :], down[...])
        sig = jax.nn.sigmoid(g)
        act = g * sig
        h = (act * u).astype(bf16)
        dg = (dh * u * sig * (1.0 + g * (1.0 - sig))).astype(bf16)
        du = (dh * act).astype(bf16)
        hid[at, :] = h
        dgate[at, :] = dg
        dup[at, :] = du
        out_acc[at, :] += dot(h, down[...], NT)
        mid_acc[at, :] += dot(dg, gate[...], NT) + dot(du, up[...], NT)
        return carry

    lax.fori_loop(0, x_ref.shape[0] // rows, body, 0)
    size = xt_ref.shape[0] // 8
    for block in range(4):
        at = slice(2 * block * size, 2 * (block + 1) * size)
        xt = xt_ref[at, :]
        three = (dot(xt, dgate[...]), dot(xt, dup[...]), dot(cott_ref[at, :], hid[...]))
        for i, term in enumerate(three):
            term = term.astype(bf16)
            for part in range(2):
                which, row = slots[2 * block + part]
                grads[which][i, row * size : (row + 1) * size, :] = term[
                    part * size : (part + 1) * size
                ]

    @pl.when(step == steps - 1)
    def _():
        out_ref[...] = out_acc[...].astype(bf16)
        mid_ref[...] = mid_acc[...].astype(bf16)


def whole_spec(shape):
    zeros = (0,) * len(shape)
    return pl.BlockSpec(shape, lambda *_: zeros)


def single_spec(shape):
    zeros = (0,) * len(shape)
    return pl.BlockSpec(shape, lambda *_: zeros, pipeline_mode=pl.Buffered(1))


def ffn_call(x, x_t, cot, cot_t, weights):
    rows, model = x.shape
    width = weights[0].shape[2]
    tile = 256 if width % 256 == 0 else 128
    steps = width // tile
    slots, heights = grad_slots(model)
    size = model // 8
    return pl.pallas_call(
        functools.partial(ffn_kernel, len(weights), slots, steps),
        grid=(steps,),
        in_specs=[single_spec(a.shape) for a in (x, x_t, cot, cot_t)]
        + [pl.BlockSpec((3, w.shape[1], tile), lambda j: (0, 0, j)) for w in weights],
        out_specs=[single_spec((rows, model))] * 2
        + [pl.BlockSpec((3, n * size, tile), lambda j: (0, 0, j)) for n in heights],
        out_shape=[jax.ShapeDtypeStruct((rows, model), bf16)] * 2
        + [jax.ShapeDtypeStruct((3, n * size, width), bf16) for n in heights],
        scratch_shapes=[pltpu.VMEM((model, tile), bf16)] * 3
        + [pltpu.VMEM((rows, tile), bf16)] * 3
        + [pltpu.VMEM((rows, model), f32)] * 2,
        compiler_params=pltpu.CompilerParams(vmem_limit_bytes=58 * 2**20),
        cost_estimate=pl.CostEstimate(
            flops=18 * rows * model * width,
            bytes_accessed=6 * rows * model * 2 + 12 * model * width,
            transcendentals=rows * width,
        ),
        name="ffn",
    )(x, x_t, cot, cot_t, *weights)


def lanes_first():
    return lax.broadcasted_iota(jnp.int32, (1, 128), 1) < 64


def head_mean(square_terms):
    first = lanes_first()
    low = jnp.sum(jnp.where(first, square_terms, 0.0), axis=-1, keepdims=True)
    high = jnp.sum(jnp.where(first, 0.0, square_terms), axis=-1, keepdims=True)
    return jnp.where(first, low, high) * (1.0 / 64)


def partner(u):
    low = (lax.broadcasted_iota(jnp.int32, (1, 128), 1) & 63) < 32
    return jnp.where(low, -pltpu.roll(u, 96, 1), pltpu.roll(u, 32, 1))


def project(x_ref, weights, w_scr, qkv):
    fill(w_scr, weights, lambda ref: ref[0])
    members, quarters, size, model = x_ref.shape
    span = members * size
    for i in range(quarters):
        qkv[i * span : (i + 1) * span, :] = dot(x_ref[:, i].reshape(span, model), w_scr[...])


def heads_of(u, gain, cosines, sines):
    inv = lax.rsqrt(head_mean(u * u) + epsilon)
    hat = u * inv
    turned = hat * gain
    return inv, hat, turned * cosines + partner(turned) * sines


def stack_heads(block):
    return jnp.concatenate([block[:, :64], block[:, 64:]], axis=0)


def unstack_heads(turned):
    half = turned.shape[1] // 2
    return jnp.concatenate([turned[:, :half], turned[:, half:]], axis=0).T


BLOCK = 256


def probs_of(q2, keys, block):
    parts = []
    for at in range(block + 1):
        parts.append(dot(keys[at * BLOCK : (at + 1) * BLOCK, :], q2, NT))
    key_at = lax.broadcasted_iota(jnp.int32, parts[-1].shape, 0)
    query_at = lax.broadcasted_iota(jnp.int32, parts[-1].shape, 1) & (BLOCK - 1)
    parts[-1] = jnp.where(key_at <= query_at, parts[-1], -1e30)
    top = functools.reduce(jnp.maximum, [jnp.max(p, axis=0, keepdims=True) for p in parts])
    parts = [jnp.exp(p - top) for p in parts]
    total = functools.reduce(jnp.add, [jnp.sum(p, axis=0, keepdims=True) for p in parts])
    inv = 1.0 / total
    return [p * inv for p in parts]


def natural_store(ref, block, value):
    members, quarters, size, _ = ref.shape
    span = members * size
    for at in range(0, BLOCK, size):
        row = block * BLOCK + at
        ref[(row % span) // size, row // span] = value[at : at + size]


def natural_load(ref, block):
    members, quarters, size, _ = ref.shape
    span = members * size
    parts = []
    for at in range(0, BLOCK, size):
        row = block * BLOCK + at
        parts.append(ref[(row % span) // size, row // span])
    return jnp.concatenate(parts, axis=0)


def attention_kernel(blocks, x_ref, cos_ref, sin_ref, qg_ref, kg_ref, *rest):
    weights, rest = rest[:blocks], rest[blocks:]
    mixed_ref, w_scr, qkv, q_scr, k_scr, vt_scr = rest
    project(x_ref, weights, w_scr, qkv)
    cosines, sines = cos_ref[...], sin_ref[...]
    _, _, q = heads_of(qkv[:, :128], qg_ref[...], cosines, sines)
    q_scr[...] = q.astype(bf16) * jnp.asarray(0.125, bf16)
    _, _, k = heads_of(qkv[:, 128:], kg_ref[...], cosines, sines)
    k_scr[...] = k[:, :64].astype(bf16)
    vt_scr[...] = qkv[:, 192:].astype(bf16).T
    for block in range(q_scr.shape[0] // BLOCK):
        at = slice(block * BLOCK, (block + 1) * BLOCK)
        q2 = stack_heads(q_scr[at, :])
        probs = probs_of(q2, k_scr, block)
        total = None
        for i, p in enumerate(probs):
            term = dot(vt_scr[:, i * BLOCK : (i + 1) * BLOCK], p.astype(bf16))
            total = term if total is None else total + term
        natural_store(mixed_ref, block, unstack_heads(total).astype(bf16))


def attention_back_kernel(blocks, slots, steps, x_ref, xt_ref, cos_ref, sin_ref, qg_ref, kg_ref, dm_ref, *rest):
    weights, rest = rest[:blocks], rest[blocks:]
    outs = max(o for o, _ in slots) + 1
    din_ref, gains_ref = rest[:2]
    grads = rest[2 : 2 + outs]
    w_scr, qkv, q_scr, k_scr, v_scr, kt_scr, dq_scr, dkv_scr, dqkv, din_acc = rest[2 + outs :]
    step = pl.program_id(0)
    project(x_ref, weights, w_scr, qkv)
    cosines, sines = cos_ref[...], sin_ref[...]
    q_gain, k_gain = qg_ref[...], kg_ref[...]
    q_inv, q_hat, q = heads_of(qkv[:, :128], q_gain, cosines, sines)
    q_scr[...] = q.astype(bf16) * jnp.asarray(0.125, bf16)
    k_inv, k_hat, k = heads_of(qkv[:, 128:], k_gain, cosines, sines)
    k_scr[...] = k[:, :64].astype(bf16)
    kt_scr[...] = k[:, :64].astype(bf16).T
    v_scr[...] = qkv[:, 192:].astype(bf16)
    dkv_scr[...] = jnp.zeros_like(dkv_scr)
    for block in range(q_scr.shape[0] // BLOCK):
        at = slice(block * BLOCK, (block + 1) * BLOCK)
        q2 = stack_heads(q_scr[at, :])
        do2 = stack_heads(natural_load(dm_ref, block))
        probs = probs_of(q2, k_scr, block)
        backs = [
            dot(v_scr[i * BLOCK : (i + 1) * BLOCK, :], do2, NT) for i in range(block + 1)
        ]
        delta = functools.reduce(
            jnp.add, [jnp.sum(p * b, axis=0, keepdims=True) for p, b in zip(probs, backs)]
        )
        total = None
        for i, (p, b) in enumerate(zip(probs, backs)):
            ds = (p * (b - delta)).astype(bf16)
            keys = slice(i * BLOCK, (i + 1) * BLOCK)
            term = dot(kt_scr[:, keys], ds)
            total = term if total is None else total + term
            dkv_scr[keys, :] += jnp.concatenate([dot(ds, q2), dot(p.astype(bf16), do2)], axis=1)
        dq_scr[at, :] = unstack_heads(total) * 0.125
    first = lanes_first()
    dq = dq_scr[...].astype(bf16).astype(f32)
    dkv = dkv_scr[...].astype(bf16).astype(f32)
    dq = dq * cosines - partner(dq) * sines
    dk = dkv * cosines - partner(dkv) * sines
    q_part = jnp.sum(dq * q_hat, axis=0, keepdims=True)
    k_part = jnp.sum(jnp.where(first, dk * k_hat, 0.0), axis=0, keepdims=True)
    both = jnp.concatenate([q_part, k_part], axis=0)

    @pl.when(step == 0)
    def _():
        gains_ref[...] = both
        din_acc[...] = jnp.zeros_like(din_acc)

    @pl.when(step > 0)
    def _():
        gains_ref[...] += both

    scaled = dq * q_gain
    d_q = q_inv * (scaled - q_hat * head_mean(scaled * q_hat))
    scaled = dk * k_gain
    d_k = k_inv * (scaled - k_hat * head_mean(scaled * k_hat))
    d_kv = jnp.where(first, d_k, dkv)
    dall = jnp.concatenate([d_q, d_kv], axis=1).astype(bf16)
    for block in range(q_scr.shape[0] // BLOCK):
        natural_store(dqkv, block, dall[block * BLOCK : (block + 1) * BLOCK])
    rows = din_acc.shape[0]
    grad = dqkv[...].reshape(rows, 256)
    din_acc[...] += dot(grad, w_scr[...], NT)
    size = xt_ref.shape[0] // 8
    for block in range(4):
        term = dot(xt_ref[2 * block * size : 2 * (block + 1) * size, :], grad).astype(bf16)
        for part in range(2):
            which, row = slots[2 * block + part]
            grads[which][0, row * size : (row + 1) * size, :] = term[part * size : (part + 1) * size]

    @pl.when(step == steps - 1)
    def _():
        din_ref[...] = din_acc[...].astype(bf16)


def attention_cost(length, heads, model, products):
    return pl.CostEstimate(
        flops=heads * (products * 2 * length * length * 64 + 2 * length * model * 256),
        bytes_accessed=4 * length * model * 2,
        transcendentals=heads * 2 * length * length,
    )


def weight_specs(weights):
    return [pl.BlockSpec((1, w.shape[1], 256), lambda j: (j, 0, 0)) for w in weights]


def attention_call(x, cosines, sines, q_gain, k_gain, weights):
    members, quarters, size, model = x.shape
    length = members * quarters * size
    heads = weights[0].shape[0]
    return pl.pallas_call(
        functools.partial(attention_kernel, len(weights)),
        grid=(heads,),
        in_specs=[single_spec(a.shape) for a in (x, cosines, sines, q_gain, k_gain)]
        + weight_specs(weights),
        out_specs=pl.BlockSpec((members, quarters, size, 128), lambda j: (0, 0, 0, j)),
        out_shape=jax.ShapeDtypeStruct((members, quarters, size, heads * 128), bf16),
        scratch_shapes=[
            pltpu.VMEM((model, 256), bf16),
            pltpu.VMEM((length, 256), f32),
            pltpu.VMEM((length, 128), bf16),
            pltpu.VMEM((length, 64), bf16),
            pltpu.VMEM((64, length), bf16),
        ],
        compiler_params=pltpu.CompilerParams(vmem_limit_bytes=48 * 2**20),
        cost_estimate=attention_cost(length, heads, model, 4),
        name="attention",
    )(x, cosines, sines, q_gain, k_gain, *weights)


def attention_back_call(x, x_t, cosines, sines, q_gain, k_gain, d_mixed, weights):
    members, quarters, size, model = x.shape
    length = members * quarters * size
    heads = weights[0].shape[0]
    slots, heights = grad_slots(model)
    eighth = model // 8
    return pl.pallas_call(
        functools.partial(attention_back_kernel, len(weights), slots, heads),
        grid=(heads,),
        in_specs=[single_spec(a.shape) for a in (x, x_t, cosines, sines, q_gain, k_gain)]
        + [pl.BlockSpec((members, quarters, size, 128), lambda j: (0, 0, 0, j))]
        + weight_specs(weights),
        out_specs=[single_spec((length, model)), whole_spec((2, 128))]
        + [pl.BlockSpec((1, n * eighth, 256), lambda j: (j, 0, 0)) for n in heights],
        out_shape=[
            jax.ShapeDtypeStruct((length, model), bf16),
            jax.ShapeDtypeStruct((2, 128), f32),
        ]
        + [jax.ShapeDtypeStruct((heads, n * eighth, 256), bf16) for n in heights],
        scratch_shapes=[
            pltpu.VMEM((model, 256), bf16),
            pltpu.VMEM((length, 256), f32),
            pltpu.VMEM((length, 128), bf16),
            pltpu.VMEM((length, 64), bf16),
            pltpu.VMEM((length, 64), bf16),
            pltpu.VMEM((64, length), bf16),
            pltpu.VMEM((length, 128), f32),
            pltpu.VMEM((length, 128), f32),
            pltpu.VMEM((members, quarters, size, 256), bf16),
            pltpu.VMEM((length, model), f32),
        ],
        compiler_params=pltpu.CompilerParams(vmem_limit_bytes=58 * 2**20),
        cost_estimate=attention_cost(length, heads, model, 10),
        name="attention_back",
    )(x, x_t, cosines, sines, q_gain, k_gain, d_mixed, *weights)


def split_rows(full):
    slots, heights = grad_slots(full.shape[1])
    if len(heights) == 1:
        return [full]
    size = full.shape[1] // 8
    outs = [[None] * n for n in heights]
    for i, (which, row) in enumerate(slots):
        outs[which][row] = full[:, i * size : (i + 1) * size]
    return [jnp.concatenate(o, axis=1) for o in outs]


def local(
    tokens,
    positions,
    cotangent,
    q_weight,
    key_matrix,
    value_matrix,
    out_weight,
    gate_weight,
    up_weight,
    down_weight,
    attn_gain,
    ffn_gain,
    q_gain,
    k_gain,
):
    model = tokens.shape[2]
    rows_here = q_weight.shape[0]
    members = 2 * lax.axis_size("s")
    sub = lax.axis_index("s")
    at_z = lax.axis_index("z")
    q_cols, kv_cols, ff_width = q_weight.shape[1], key_matrix.shape[1], gate_weight.shape[1]
    kv_heads = kv_cols // 64
    heads_here = kv_heads // members

    per_head = jnp.concatenate(
        [
            q_weight.reshape(rows_here, kv_heads, 128),
            key_matrix.reshape(rows_here, kv_heads, 64),
            value_matrix.reshape(rows_here, kv_heads, 64),
        ],
        axis=2,
    ).transpose(1, 0, 2)

    def pair_of(array, axis):
        if members == 2:
            size = array.shape[axis] // 2
            return [lax.slice_in_dim(array, i * size, (i + 1) * size, axis=axis) for i in range(2)]
        size = array.shape[axis] // members
        return [
            lax.dynamic_slice_in_dim(array, (2 * sub + i) * size, size, axis=axis) for i in range(2)
        ]

    qkv_blocks = gather_rows(pair_of(per_head, 0))
    out_blocks = gather_rows(pair_of(out_weight[None], 2))
    chunks = 3
    trio = [pair_of(w, 1) for w in (gate_weight, up_weight, down_weight)]
    chunk_width = trio[0][0].shape[1] // chunks
    ffn_blocks = []
    for k in range(chunks):
        cols = slice(k * chunk_width, (k + 1) * chunk_width)
        ffn_blocks.append(
            gather_rows([jnp.stack([w[i][:, cols] for w in trio], axis=0) for i in range(2)])
        )

    tok = to_sequence(relative(tokens))
    quarters, size, _ = tok.shape
    own = quarters * size
    length = own * members
    tok = tok.reshape(own, model).astype(f32)
    attn_gain_r = relative(attn_gain)
    ffn_gain_r = relative(ffn_gain)
    in_scale = rms_scale(tok)
    in_hat = tok * in_scale
    x = group_gather((in_hat * attn_gain_r).astype(bf16))
    x4 = x.reshape(members, quarters, size, model)

    cot = to_sequence(relative(cotangent)).reshape(own, model)
    cot_full = group_gather(cot).reshape(length, model)
    cot_t = cot_full.T

    every_pos = lax.all_gather(positions, ("z", "s", "c"), axis=0)
    every_pos = every_pos.reshape(quarters, members // 2, 4, 2 * size)
    pos = lax.dynamic_index_in_dim(every_pos, at_z, axis=2, keepdims=False).reshape(length)
    inverse = rope_base ** (-(2.0 * jnp.arange(32, dtype=f32)) / 64)
    turned = pos.astype(f32)[:, None] * inverse[None, :]
    cosines = jnp.tile(jnp.cos(turned), (1, 4))
    sines = jnp.tile(jnp.sin(turned), (1, 4))
    q_gain2 = jnp.tile(q_gain, 2)[None]
    k_gain2 = jnp.tile(k_gain, 2)[None]

    mixed = attention_call(x4, cosines, sines, q_gain2, k_gain2, qkv_blocks)
    mixed = mixed.reshape(length, heads_here * 128)
    out_w = jnp.concatenate([b[0] for b in out_blocks], axis=0)
    partial = dot(mixed, out_w, NT).astype(bf16).reshape(members, own, model)
    residual = tok + group_scatter([partial])
    mid_scale = rms_scale(residual)
    mid_hat = residual * mid_scale
    mid = group_gather((mid_hat * ffn_gain_r).astype(bf16)).reshape(length, model)
    mid_t = mid.T

    out_parts, mid_parts, ffn_sums = [], [], []
    for k in range(chunks):
        out_part, mid_part, *grads = ffn_call(mid, mid_t, cot_full, cot_t, ffn_blocks[k])
        out_parts.append(out_part.reshape(members, own, model))
        mid_parts.append(mid_part.reshape(members, own, model))
        ffn_sums.append(reduce_rows(grads))

    d_mid = group_scatter(mid_parts)
    ffn_gain_part = jnp.sum(d_mid * mid_hat, axis=0)
    d_resid = cot.astype(f32) + norm_back(d_mid, mid_hat, mid_scale, ffn_gain_r)
    d_attn = group_gather(d_resid.astype(bf16)).reshape(length, model)
    d_mixed = dot(d_attn, out_w).astype(bf16)
    d_mixed = d_mixed.reshape(members, quarters, size, heads_here * 128)
    out_term = lax.dot_general(
        d_attn, mixed, (((0,), (0,)), ((), ())), preferred_element_type=f32
    ).astype(bf16)
    out_sum = reduce_rows(split_rows(out_term[None]))

    x_t = x.reshape(length, model).T
    d_in_part, head_gains, *grads = attention_back_call(
        x4, x_t, cosines, sines, q_gain2, k_gain2, d_mixed, qkv_blocks
    )
    qkv_sum = reduce_rows(grads)
    d_in = group_scatter([d_in_part.reshape(members, own, model)])
    attn_gain_part = jnp.sum(d_in * in_hat, axis=0)
    input_grad = d_resid + norm_back(d_in, in_hat, in_scale, attn_gain_r)
    input_grad = relative(input_grad.astype(bf16).reshape(quarters, size, model))
    input_grad = from_sequence(input_grad)

    output = (residual + group_scatter(out_parts)).astype(bf16)
    output = from_sequence(relative(output.reshape(quarters, size, model)))

    gain_terms = jnp.concatenate(
        [
            relative(attn_gain_part),
            relative(ffn_gain_part),
            head_gains[0, :64] + head_gains[0, 64:],
            head_gains[1, :64],
        ]
    )
    gain_sums = lax.psum(gain_terms, EVERY)

    heads = jnp.concatenate(qkv_sum, axis=0).transpose(1, 0, 2).astype(f32)
    ffn_grads = [
        jnp.concatenate(
            [ffn_sums[k][i][w] for i in range(members) for k in range(chunks)], axis=1
        ).astype(f32)
        for w in range(3)
    ]
    return (
        output,
        input_grad,
        heads[:, :, :128].reshape(rows_here, q_cols),
        heads[:, :, 128:192].reshape(rows_here, kv_cols),
        heads[:, :, 192:].reshape(rows_here, kv_cols),
        jnp.concatenate([o[0] for o in out_sum], axis=1).astype(f32),
        ffn_grads[0],
        ffn_grads[1],
        ffn_grads[2],
        gain_sums[:model],
        gain_sums[model : 2 * model],
        gain_sums[2 * model : 2 * model + 64],
        gain_sums[2 * model + 64 :],
    )


def solution(mesh):
    dp, seq = mesh.devices.shape
    lines = 4
    fine = Mesh(mesh.devices.reshape(dp // 4, 2, 2, lines, seq // lines), EVERY)
    rows, cols = ("o", "x", "c"), ("z", "s")
    tokens = P(rows, cols, None)
    weight = P(rows, None)
    return jax.shard_map(
        local,
        mesh=fine,
        in_specs=(tokens, P(rows, cols), tokens) + (weight,) * 7 + (P(),) * 4,
        out_specs=(tokens, tokens) + (weight,) * 7 + (P(),) * 4,
        check_vma=False,
    )
```

```python
import functools

import jax
import jax.numpy as jnp
from jax import lax
from jax.experimental import pallas as pl
from jax.experimental.pallas import tpu as pltpu
from jax.sharding import Mesh, PartitionSpec as P

epsilon = 1e-05
rope_base = 1000000.0
f32 = jnp.float32
bf16 = jnp.bfloat16
SWAP = ((0, 1), (1, 0))
EVERY = ("o", "x", "c", "z", "s")
NT = (((1,), (1,)), ((), ()))
NN = (((1,), (0,)), ((), ()))


def dot(left, right, dims=NN):
    return lax.dot_general(left, right, dims, preferred_element_type=f32)


def rms_scale(rows):
    return lax.rsqrt(jnp.mean(rows * rows, axis=-1, keepdims=True) + epsilon)


def norm_back(grad_out, normed_hat, inv_scale, gain):
    scaled = grad_out * gain
    return inv_scale * (scaled - normed_hat * jnp.mean(scaled * normed_hat, axis=-1, keepdims=True))


def square():
    return lax.axis_size("o") == 2 and lax.axis_size("x") == 2


def pair_group():
    return lax.axis_size("s") == 1


def chip_at():
    if not square():
        return jnp.int32(0)
    return 2 * lax.axis_index("o") + lax.axis_index("x")


def flip_at():
    return lax.axis_index("c") if pair_group() else jnp.int32(0)


def relative(vector):
    if not square():
        return vector
    quarter = vector.shape[0] // 4
    blocks = [
        lax.dynamic_slice_in_dim(vector, (chip_at() ^ i) * quarter, quarter) for i in range(4)
    ]
    return jnp.concatenate(blocks)


def after(array, *others):
    return lax.optimization_barrier((array, *others))[0]


def swap_core(array):
    return lax.ppermute(array, "c", SWAP)


def group_gather(rows):
    if pair_group():
        return [rows, swap_core(rows)]
    full = lax.all_gather(rows, ("s", "c"), axis=0)
    return [full[i] for i in range(full.shape[0])]


def group_scatter(parts):
    if pair_group():
        away = sum(p[1].astype(f32) for p in parts).astype(bf16)
        return sum(p[0].astype(f32) for p in parts) + swap_core(away).astype(f32)
    total = jnp.stack([sum(p[m].astype(f32) for p in parts) for m in range(len(parts[0]))])
    return lax.psum_scatter(total, ("s", "c"), scatter_dimension=0, tiled=False)


def merge_kernel(relate, at_ref, mine_ref, other_ref, out_ref):
    core, chip = at_ref[0], at_ref[1]
    if not relate:
        out_ref[:, core] = mine_ref[...]
        out_ref[:, 1 - core] = other_ref[...]
        return
    quarter = mine_ref.shape[-1] // 4
    for r in range(4):
        to = pl.ds(pl.multiple_of((chip ^ r) * quarter, quarter), quarter)
        at = slice(r * quarter, (r + 1) * quarter)
        out_ref[:, core, :, to] = mine_ref[:, :, at]
        out_ref[:, 1 - core, :, to] = other_ref[:, :, at]


def smem():
    return pl.BlockSpec(memory_space=pltpu.SMEM)


def place():
    return jnp.stack([lax.axis_index("c"), chip_at()]).astype(jnp.int32)


def small_cost(bytes_moved):
    return pl.CostEstimate(flops=0, bytes_accessed=bytes_moved, transcendentals=0)


def by_core(mine, other, relate=False):
    n, rows, width = mine.shape
    step = 1 if n % 3 else n // 3
    block = pl.BlockSpec((step, rows, width), lambda i: (i, 0, 0))
    out = pl.pallas_call(
        functools.partial(merge_kernel, relate),
        grid=(n // step,),
        in_specs=[smem(), block, block],
        out_specs=pl.BlockSpec((step, 2, rows, width), lambda i: (i, 0, 0, 0)),
        out_shape=jax.ShapeDtypeStruct((n, 2, rows, width), mine.dtype),
        cost_estimate=small_cost(mine.size * 8),
        compiler_params=pltpu.CompilerParams(vmem_limit_bytes=32 * 2**20),
        name="merge",
    )(place(), mine, other)
    return out.reshape(n, 2 * rows, width)


def enter_kernel(at_ref, rows_ref, *refs):
    core, chip = at_ref[0], at_ref[1]
    mine_ref, away_ref = refs[-2:]
    size = mine_ref.shape[1]
    model = rows_ref.shape[-1]
    quarter = model // 4
    for ref, which in ((mine_ref, core), (away_ref, 1 - core)):
        span = pl.ds(pl.multiple_of(which * size, size), size)
        for r in range(4):
            at = pl.ds(pl.multiple_of((chip ^ r) * quarter, quarter), quarter)
            ref[:, :, r * quarter : (r + 1) * quarter] = rows_ref[:, span, at]
        if len(refs) == 3:
            ref[:, :, model:] = refs[0][:, span, :]


def to_sequence(rows, *extra):
    seqs, count, width = rows.shape
    width += sum(e.shape[2] for e in extra)
    half = jax.ShapeDtypeStruct((seqs, count // 2, width), rows.dtype)
    mine, away = pl.pallas_call(
        enter_kernel,
        in_specs=[smem()] + [pl.BlockSpec(memory_space=pltpu.VMEM)] * (1 + len(extra)),
        out_specs=[pl.BlockSpec(memory_space=pltpu.VMEM)] * 2,
        out_shape=[half, half],
        cost_estimate=small_cost(rows.size * 4),
        name="enter",
    )(place(), rows, *extra)
    other = swap_core(away)
    every = by_core(mine.reshape(1, -1, width), other.reshape(1, -1, width))
    return lax.all_to_all(every.reshape(2 * seqs, count // 2, width), "z", 0, 0, tiled=True)


def from_sequence(rows):
    core = lax.axis_index("c")
    every = lax.all_to_all(rows, "z", 0, 0, tiled=True)
    seqs = every.shape[0] // 2
    away = lax.dynamic_slice_in_dim(every, (1 - core) * seqs, seqs)
    mine = lax.dynamic_slice_in_dim(every, core * seqs, seqs)
    return by_core(mine, swap_core(away), relate=True)


def pair_kernel(at_ref, mine_ref, other_ref, out_ref):
    core = at_ref[0]
    out_ref[core] = mine_ref[...]
    out_ref[1 - core] = other_ref[...]


def core_pair(mine, other, tile, start, count):
    n, rows, _ = mine.shape
    block = pl.BlockSpec((n, rows, tile), lambda i: (0, 0, start + i))
    return pl.pallas_call(
        pair_kernel,
        grid=(count,),
        in_specs=[smem(), block, block],
        out_specs=pl.BlockSpec((2, n, rows, tile), lambda i: (0, 0, 0, i)),
        out_shape=jax.ShapeDtypeStruct((2, n, rows, count * tile), mine.dtype),
        cost_estimate=small_cost(8 * n * rows * count * tile),
        name="core_pair",
    )(place(), mine, other)


class Gather:
    def __init__(self, own, *before):
        self.own = own
        if square():
            own = after(own, *before)
            self.first = [lax.ppermute(own, "x", SWAP), lax.ppermute(own, "o", SWAP)]
            by_x, by_o = self.first
            self.second = [
                lax.ppermute(by_x[:1], "o", SWAP),
                lax.ppermute(by_o[1:], "x", SWAP),
            ]
        else:
            self.first = self.second = []

    def blocks(self):
        if square():
            return [self.own, *self.first, *self.second]
        full = lax.all_gather(self.own, ("o", "x"), axis=0, tiled=True)
        return [full[i : i + 2] for i in range(0, full.shape[0], 2)]


def grad_slots(model):
    if square():
        return [(2, 0), (3, 0), (0, 0), (3, 1), (2, 1), (1, 0), (0, 1), (1, 1)], [2, 2, 2, 2]
    return [(0, i) for i in range(8)], [8]


def put_rows(out_refs, slots, index, cols, term):
    size = term.shape[0] // 8
    for part, (which, row) in enumerate(slots):
        out_refs[which][index, row * size : (row + 1) * size, cols] = term[
            part * size : (part + 1) * size
        ].astype(bf16)


def add_up(*terms):
    return functools.reduce(jnp.add, [t.astype(f32) for t in terms]).astype(bf16)


def combine_kernel(keep_a, come_a, last_a, keep_b, come_b, last_b, out_ref):
    half = last_a.shape[1]
    for at, (keep, come, last) in enumerate(((keep_a, come_a, last_a), (keep_b, come_b, last_b))):
        out_ref[:, at * half : (at + 1) * half, :] = add_up(keep[...], come[...], last[...])


def combine(keep_a, come_a, last_a, keep_b, come_b, last_b):
    n, half, width = last_a.shape
    block = pl.BlockSpec((1, half, width), lambda i: (i, 0, 0))
    return pl.pallas_call(
        combine_kernel,
        grid=(n,),
        in_specs=[block] * 6,
        out_specs=pl.BlockSpec((1, 2 * half, width), lambda i: (i, 0, 0)),
        out_shape=jax.ShapeDtypeStruct((n, 2 * half, width), bf16),
        cost_estimate=small_cost(16 * n * half * width),
        name="combine",
    )(keep_a, come_a, last_a, keep_b, come_b, last_b)


class Reduction:
    def __init__(self, outs):
        self.step = 0
        self.state = outs
        if square():
            self.state = [
                *outs,
                lax.ppermute(outs[0], "x", SWAP),
                lax.ppermute(outs[1], "o", SWAP),
            ]

    def advance(self):
        step, self.step = self.step, self.step + 1
        state = self.state
        on_line = lax.axis_size("z") == 4
        if step == 0 and square():
            _, _, keep_a, keep_b, come_a, come_b = state
            half = keep_a.shape[1] // 2
            go_a = add_up(keep_a[:, half:], come_a[:, half:])
            go_b = add_up(keep_b[:, half:], come_b[:, half:])
            last_a, last_b = lax.ppermute(go_a, "o", SWAP), lax.ppermute(go_b, "x", SWAP)
            self.state = (keep_a, come_a, last_a, keep_b, come_b, last_b)
            return [go_a, go_b]
        if step == 1:
            if square():
                here = combine(*state)
            else:
                here = lax.psum_scatter(
                    state[0].astype(f32), ("o", "x"), scatter_dimension=1, tiled=True
                ).astype(bf16)
            come = lax.ppermute(here, "z", ((0, 1), (3, 2))) if on_line else None
            self.state = (here, come)
            return [here]
        if step == 2 and on_line:
            here = add_up(*state)
            self.state = (here, lax.ppermute(here, "z", ((1, 2), (2, 1))))
            return [here]
        if step == 3 and on_line:
            here = add_up(*state)
            self.state = (here, lax.ppermute(here, "z", ((1, 0), (2, 3))))
            return [here]
        if step == 4:
            if on_line:
                at = lax.axis_index("z")
                total = jnp.where((at == 0) | (at == 3), state[1], state[0])
            else:
                total = lax.psum(state[0].astype(f32), "z").astype(bf16)
            core = lax.axis_index("c")
            half = total.shape[1] // 2
            mine = lax.dynamic_slice_in_dim(total, core * half, half, 1)
            away = lax.dynamic_slice_in_dim(total, (1 - core) * half, half, 1)
            self.state = (mine, swap_core(away))
            return [total]
        return []


def every_member(done):
    mine, other = done
    first = lax.axis_index("c") == 0
    pair = jnp.stack([jnp.where(first, mine, other), jnp.where(first, other, mine)])
    every = lax.all_gather(pair, "s", axis=0, tiled=True)
    return [every[i] for i in range(every.shape[0])]


def sum_all(terms, before):
    if not (square() and pair_group() and lax.axis_size("z") == 4):
        return lax.psum(terms, EVERY)
    for axis, perm in (
        ("c", SWAP),
        ("x", SWAP),
        ("o", SWAP),
        ("z", ((0, 1), (1, 0), (2, 3), (3, 2))),
        ("z", ((0, 2), (2, 0), (1, 3), (3, 1))),
    ):
        if axis == "z":
            terms = after(terms, before)
        terms = terms + lax.ppermute(terms, axis, perm)
    return terms


def member_cols(start, count):
    return pl.ds(pl.multiple_of(start, 128), count)


def pack_attn_kernel(heads, at_ref, q_ref, k_ref, v_ref, o_ref, *outs):
    for i in range(2):
        member, attn_ref = at_ref[i], outs[i]
        for j in range(0, heads, 2):
            head = member * heads + j
            keys = k_ref[:, member_cols(head * 64, 128)]
            values = v_ref[:, member_cols(head * 64, 128)]
            for m in range(2):
                attn_ref[j + m, :, :128] = q_ref[:, member_cols((head + m) * 128, 128)]
                attn_ref[j + m, :, 128:192] = keys[:, m * 64 : (m + 1) * 64]
                attn_ref[j + m, :, 192:] = values[:, m * 64 : (m + 1) * 64]
        for j in range(heads // 2):
            attn_ref[heads + j] = o_ref[:, member_cols(member * heads * 128 + j * 256, 256)]


def pack_ffn_kernel(at_ref, g_ref, u_ref, d_ref, *outs):
    for i in range(2):
        width = outs[i].shape[2]
        for w, ref in enumerate((g_ref, u_ref, d_ref)):
            outs[i][w] = ref[:, member_cols(at_ref[i] * width, width)]


def pack_call(kernel, members_at, out, weights):
    return pl.pallas_call(
        kernel,
        in_specs=[smem()] + [pl.BlockSpec(memory_space=pltpu.VMEM)] * len(weights),
        out_specs=[pl.BlockSpec(memory_space=pltpu.VMEM)] * 2,
        out_shape=[jax.ShapeDtypeStruct(out, bf16)] * 2,
        cost_estimate=small_cost(2 * 4 * out[0] * out[1] * out[2]),
        compiler_params=pltpu.CompilerParams(vmem_limit_bytes=32 * 2**20),
        name="pack",
    )(members_at, *weights)


def finish_ffn_kernel(at_ref, *refs):
    mines, others, outs = refs[:-3:2], refs[1:-3:2], refs[-3:]
    first = at_ref[0] == 0
    total = sum(m.shape[2] for m in mines)
    start = 0
    for mine_ref, other_ref in zip(mines, others):
        width = mine_ref.shape[2]
        mine, other = mine_ref[0], other_ref[0]
        low = jnp.where(first, mine, other).astype(f32)
        high = jnp.where(first, other, mine).astype(f32)
        for w in range(3):

            @pl.when(pl.program_id(0) == w)
            def _():
                outs[w][:, start : start + width] = low
                outs[w][:, total + start : total + start + width] = high

        start += width


def finish_ffn_call(sums):
    rows = sums[0][0].shape[1]
    out = jax.ShapeDtypeStruct((rows, 2 * sum(s[0].shape[2] for s in sums)), f32)
    arrays = [a for s in sums for a in s]
    return pl.pallas_call(
        finish_ffn_kernel,
        grid=(3,),
        in_specs=[smem()] + [pl.BlockSpec((1, *a.shape[1:]), lambda w: (w, 0, 0)) for a in arrays],
        out_specs=[whole_spec(out.shape)] * 3,
        out_shape=[out] * 3,
        cost_estimate=small_cost(out.size * 18),
        compiler_params=pltpu.CompilerParams(vmem_limit_bytes=40 * 2**20),
        name="finish_ffn",
    )(place(), *arrays)


def finish_heads_kernel(calls, at_ref, *refs):
    first = at_ref[0] == 0
    q_ref, k_ref, v_ref, o_ref = refs[2 * calls :]
    per_call = refs[0].shape[0]
    heads = calls * per_call

    def pick(head):
        mine, other = refs[2 * (head // per_call)], refs[2 * (head // per_call) + 1]
        mine, other = mine[head % per_call], other[head % per_call]
        return [
            jnp.where(first, mine, other).astype(f32),
            jnp.where(first, other, mine).astype(f32),
        ]

    for j in range(0, heads, 2):
        pairs = [pick(j), pick(j + 1)]
        for g in range(2):
            pair = [p[g] for p in pairs]
            head = g * heads + j
            for m in range(2):
                at = slice((head + m) * 128, (head + m + 1) * 128)
                q_ref[:, at] = pair[m][:, :128]
                o_ref[:, at] = pair[m][:, 256:]
            at = slice(head * 64, (head + 2) * 64)
            k_ref[:, at] = jnp.concatenate([p[:, 128:192] for p in pair], axis=1)
            v_ref[:, at] = jnp.concatenate([p[:, 192:256] for p in pair], axis=1)


def finish_heads_call(heads_sums):
    per_call, rows, _ = heads_sums[0][0].shape
    heads = per_call * len(heads_sums)
    wide = jax.ShapeDtypeStruct((rows, heads * 256), f32)
    narrow = jax.ShapeDtypeStruct((rows, heads * 128), f32)
    return pl.pallas_call(
        functools.partial(finish_heads_kernel, len(heads_sums)),
        in_specs=[smem()] + [pl.BlockSpec(memory_space=pltpu.VMEM)] * (2 * len(heads_sums)),
        out_specs=[pl.BlockSpec(memory_space=pltpu.VMEM)] * 4,
        out_shape=[wide, narrow, narrow, wide],
        cost_estimate=small_cost(rows * heads * 768 * 6),
        name="finish_heads",
    )(place(), *[a for s in heads_sums for a in s])


def fill(scratch, refs, index):
    row = 0
    for ref in refs:
        for part in range(ref.shape[0]):
            block = ref[part, index]
            scratch[row : row + block.shape[0], :] = block
            row += block.shape[0]


def ffn_kernel(members, blocks, slots, steps, *refs):
    xs, xts, cots, cotts = [refs[i * members : (i + 1) * members] for i in range(4)]
    rest = refs[4 * members :]
    weights, rest = rest[:blocks], rest[blocks:]
    out_refs, mid_refs = rest[:members], rest[members : 2 * members]
    grads = rest[2 * members : -8]
    gate, up, down, hid, dgate, dup, out_acc, mid_acc = rest[-8:]
    step = pl.program_id(0)
    for i, scratch in enumerate((gate, up, down)):
        fill(scratch, weights, i)

    @pl.when(step == 0)
    def _():
        out_acc[...] = jnp.zeros_like(out_acc)
        mid_acc[...] = jnp.zeros_like(mid_acc)

    own = xs[0].shape[0]
    rows = 512
    for m in range(members):

        def body(i, carry):
            at = pl.ds(pl.multiple_of(i * rows, rows), rows)
            to = pl.ds(pl.multiple_of(m * own + i * rows, rows), rows)
            x = xs[m][at, :]
            g = dot(x, gate[...])
            u = dot(x, up[...])
            dh = dot(cots[m][at, :], down[...])
            sig = jax.nn.sigmoid(g)
            act = g * sig
            h = (act * u).astype(bf16)
            dg = (dh * u * sig * (1.0 + g * (1.0 - sig))).astype(bf16)
            du = (dh * act).astype(bf16)
            hid[to, :] = h
            dgate[to, :] = dg
            dup[to, :] = du
            out_acc[to, :] += dot(h, down[...], NT)
            mid_acc[to, :] += dot(dg, gate[...], NT) + dot(du, up[...], NT)
            return carry

        lax.fori_loop(0, own // rows, body, 0)

    def over_rows(lefts, at, right):
        return functools.reduce(
            jnp.add,
            [dot(l[at, :], right[m * own : (m + 1) * own, :]) for m, l in enumerate(lefts)],
        )

    model = xts[0].shape[0]
    for i, (lefts, right) in enumerate(((xts, dgate), (xts, dup), (cotts, hid))):
        term = over_rows(lefts, slice(0, model), right)
        put_rows(grads, slots, i, slice(None), term)

    @pl.when(step == steps - 1)
    def _():
        for m in range(members):
            out_refs[m][...] = out_acc[m * own : (m + 1) * own, :].astype(bf16)
            mid_refs[m][...] = mid_acc[m * own : (m + 1) * own, :].astype(bf16)


def turn_kernel(in_ref, out_ref):
    out_ref[...] = in_ref[...].T


def turn(rows, width):
    count = rows.shape[0]
    return pl.pallas_call(
        turn_kernel,
        grid=(2,),
        in_specs=[pl.BlockSpec((count, width // 2), lambda i: (0, i))],
        out_specs=pl.BlockSpec((width // 2, count), lambda i: (i, 0)),
        out_shape=jax.ShapeDtypeStruct((width, count), rows.dtype),
        cost_estimate=small_cost(rows.size * 4),
        name="turn",
    )(rows)


def whole_spec(shape):
    zeros = (0,) * len(shape)
    return pl.BlockSpec(shape, lambda *_: zeros)


def single_spec(shape):
    zeros = (0,) * len(shape)
    return pl.BlockSpec(shape, lambda *_: zeros, pipeline_mode=pl.Buffered(1))


SHARE = 32

CHUNKS = (3, 3, 3)


def ffn_call(tile, steps, x, x_t, cot, cot_t, weights):
    members = len(x)
    own, model = x[0].shape
    rows = own * members
    width = steps * tile
    slots, heights = grad_slots(model)
    size = model // 8
    return pl.pallas_call(
        functools.partial(ffn_kernel, members, len(weights), slots, steps),
        grid=(steps,),
        in_specs=[single_spec((own, model))] * members
        + [single_spec(a.shape) for a in (*x_t, *cot, *cot_t)]
        + [
            pl.BlockSpec((w.shape[0], 3, w.shape[2], tile), lambda j: (0, 0, 0, j))
            for w in weights
        ],
        out_specs=[single_spec((own, model))] * (2 * members)
        + [pl.BlockSpec((3, n * size, tile), lambda j: (0, 0, j)) for n in heights],
        out_shape=[jax.ShapeDtypeStruct((own, model), bf16)] * (2 * members)
        + [jax.ShapeDtypeStruct((3, n * size, width), bf16) for n in heights],
        scratch_shapes=[pltpu.VMEM((model, tile), bf16)] * 3
        + [pltpu.VMEM((rows, tile), bf16)] * 3
        + [pltpu.VMEM((rows, model), f32)] * 2,
        compiler_params=pltpu.CompilerParams(vmem_limit_bytes=58 * 2**20),
        cost_estimate=pl.CostEstimate(
            flops=18 * rows * model * width // SHARE,
            bytes_accessed=(6 * rows * model * 2 + 12 * model * width) // SHARE,
            transcendentals=rows * width // SHARE,
        ),
        name="ffn",
    )(*x, *x_t, *cot, *cot_t, *weights)


def lanes_first():
    return lax.broadcasted_iota(jnp.int32, (1, 128), 1) < 64


def head_mean(square_terms):
    first = lanes_first()
    low = jnp.sum(jnp.where(first, square_terms, 0.0), axis=-1, keepdims=True)
    high = jnp.sum(jnp.where(first, 0.0, square_terms), axis=-1, keepdims=True)
    return jnp.where(first, low, high) * (1.0 / 64)


def partner(u):
    low = (lax.broadcasted_iota(jnp.int32, (1, 128), 1) & 63) < 32
    return jnp.where(low, -pltpu.roll(u, 96, 1), pltpu.roll(u, 32, 1))


def natural_rows(flip, members, own, size):
    for m in range(members):
        for i in range(own // size):
            to = pl.multiple_of((i * members + (m ^ flip)) * size, size)
            yield m, i * size, pl.ds(to, size)


def project(flip, size, xs, weights, w_scr, qkv):
    fill(w_scr, weights, 0)
    own = xs[0].shape[0]
    terms = [dot(x[...], w_scr[...]) for x in xs]
    for m, row, at in natural_rows(flip, len(xs), own, size):
        qkv[at, :] = terms[m][row : row + size]


def heads_of(u, gain, cosines, sines):
    inv = lax.rsqrt(head_mean(u * u) + epsilon)
    hat = u * inv
    turned = hat * gain
    return inv, hat, turned * cosines + partner(turned) * sines


def stack_heads(block):
    return jnp.concatenate([block[:, :64], block[:, 64:]], axis=0)


def unstack_heads(turned):
    half = turned.shape[1] // 2
    return jnp.concatenate([turned[:, :half], turned[:, half:]], axis=0).T


BLOCK = 256


def probs_of(q2, keys, block):
    parts = []
    for at in range(block + 1):
        parts.append(dot(keys[at * BLOCK : (at + 1) * BLOCK, :], q2, NT))
    key_at = lax.broadcasted_iota(jnp.int32, parts[-1].shape, 0)
    query_at = lax.broadcasted_iota(jnp.int32, parts[-1].shape, 1) & (BLOCK - 1)
    parts[-1] = jnp.where(key_at <= query_at, parts[-1], -1e30)
    top = functools.reduce(jnp.maximum, [jnp.max(p, axis=0, keepdims=True) for p in parts])
    parts = [jnp.exp(p - top) for p in parts]
    total = functools.reduce(jnp.add, [jnp.sum(p, axis=0, keepdims=True) for p in parts])
    inv = 1.0 / total
    return [p * inv for p in parts]


def attention_kernel(members, blocks, size, at_ref, *refs):
    xs, rest = refs[:members], refs[members:]
    cos_ref, sin_ref, qg_ref, kg_ref = rest[:4]
    weights, rest = rest[4 : 4 + blocks], rest[4 + blocks :]
    mixed_refs, rest = rest[:members], rest[members:]
    w_scr, qkv, q_scr, k_scr, vt_scr, mixed_scr = rest
    flip = at_ref[0]
    project(flip, size, xs, weights, w_scr, qkv)
    cosines, sines = cos_ref[...], sin_ref[...]
    _, _, q = heads_of(qkv[:, :128], qg_ref[...], cosines, sines)
    q_scr[...] = q.astype(bf16) * jnp.asarray(0.125, bf16)
    _, _, k = heads_of(qkv[:, 128:], kg_ref[...], cosines, sines)
    k_scr[...] = k[:, :64].astype(bf16)
    vt_scr[...] = qkv[:, 192:].astype(bf16).T
    for block in range(q_scr.shape[0] // BLOCK):
        at = slice(block * BLOCK, (block + 1) * BLOCK)
        q2 = stack_heads(q_scr[at, :])
        probs = probs_of(q2, k_scr, block)
        total = None
        for i, p in enumerate(probs):
            term = dot(vt_scr[:, i * BLOCK : (i + 1) * BLOCK], p.astype(bf16))
            total = term if total is None else total + term
        mixed_scr[at, :] = unstack_heads(total).astype(bf16)
    for m, row, at in natural_rows(flip, members, xs[0].shape[0], size):
        mixed_refs[m][row : row + size, :] = mixed_scr[at, :]


def attention_back_kernel(members, blocks, slots, steps, size, at_ref, *refs):
    xs, xts, das, mixes = [refs[i * members : (i + 1) * members] for i in range(4)]
    rest = refs[4 * members :]
    cos_ref, sin_ref, qg_ref, kg_ref = rest[:4]
    dms, rest = rest[4 : 4 + members], rest[4 + members :]
    weights, rest = rest[:blocks], rest[blocks:]
    din_refs, gains_ref, grads = rest[:members], rest[members], rest[members + 1 : -12]
    rest = rest[-12:]
    w_scr, qkv, q_scr, k_scr, v_scr, kt_scr, dm_scr, dq_scr, dkv_scr, dall, dqkv, din_acc = rest
    flip = at_ref[0]
    own = xs[0].shape[0]
    step = pl.program_id(0)
    project(flip, size, xs, weights, w_scr, qkv)
    for m, row, at in natural_rows(flip, members, own, size):
        dm_scr[at, :] = dms[m][row : row + size, :]
    cosines, sines = cos_ref[...], sin_ref[...]
    q_gain, k_gain = qg_ref[...], kg_ref[...]
    q_inv, q_hat, q = heads_of(qkv[:, :128], q_gain, cosines, sines)
    q_scr[...] = q.astype(bf16) * jnp.asarray(0.125, bf16)
    k_inv, k_hat, k = heads_of(qkv[:, 128:], k_gain, cosines, sines)
    k_scr[...] = k[:, :64].astype(bf16)
    kt_scr[...] = k[:, :64].astype(bf16).T
    v_scr[...] = qkv[:, 192:].astype(bf16)
    dkv_scr[...] = jnp.zeros_like(dkv_scr)
    for block in range(q_scr.shape[0] // BLOCK):
        at = slice(block * BLOCK, (block + 1) * BLOCK)
        q2 = stack_heads(q_scr[at, :])
        do2 = stack_heads(dm_scr[at, :])
        probs = probs_of(q2, k_scr, block)
        backs = [
            dot(v_scr[i * BLOCK : (i + 1) * BLOCK, :], do2, NT) for i in range(block + 1)
        ]
        delta = functools.reduce(
            jnp.add, [jnp.sum(p * b, axis=0, keepdims=True) for p, b in zip(probs, backs)]
        )
        total = None
        for i, (p, b) in enumerate(zip(probs, backs)):
            ds = (p * (b - delta)).astype(bf16)
            keys = slice(i * BLOCK, (i + 1) * BLOCK)
            term = dot(kt_scr[:, keys], ds)
            total = term if total is None else total + term
            dkv_scr[keys, :] += jnp.concatenate([dot(ds, q2), dot(p.astype(bf16), do2)], axis=1)
        dq_scr[at, :] = unstack_heads(total) * 0.125
    first = lanes_first()
    dq = dq_scr[...].astype(bf16).astype(f32)
    dkv = dkv_scr[...].astype(bf16).astype(f32)
    dq = dq * cosines - partner(dq) * sines
    dk = dkv * cosines - partner(dkv) * sines
    q_part = jnp.sum(dq * q_hat, axis=0, keepdims=True)
    k_part = jnp.sum(jnp.where(first, dk * k_hat, 0.0), axis=0, keepdims=True)
    both = jnp.concatenate([q_part, k_part], axis=0)

    @pl.when(step == 0)
    def _():
        gains_ref[...] = both
        din_acc[...] = jnp.zeros_like(din_acc)

    @pl.when(step > 0)
    def _():
        gains_ref[...] += both

    scaled = dq * q_gain
    d_q = q_inv * (scaled - q_hat * head_mean(scaled * q_hat))
    scaled = dk * k_gain
    d_k = k_inv * (scaled - k_hat * head_mean(scaled * k_hat))
    dall[:, :128] = d_q.astype(bf16)
    dall[:, 128:] = jnp.where(first, d_k, dkv).astype(bf16)
    for m, row, at in natural_rows(flip, members, own, size):
        dqkv[m * own + row : m * own + row + size, :] = dall[at, :]
    din_acc[...] += dot(dqkv[...], w_scr[...], NT)
    term = sum(dot(xt[...], dqkv[m * own : (m + 1) * own, :]) for m, xt in enumerate(xts))
    put_rows(grads, slots, 0, slice(0, 256), term)
    term = sum(dot(da[...], mix[...]) for da, mix in zip(das, mixes))
    put_rows(grads, slots, 0, slice(256, 384), term)

    @pl.when(step == steps - 1)
    def _():
        for m in range(members):
            din_refs[m][...] = din_acc[m * own : (m + 1) * own, :].astype(bf16)


def attention_cost(length, heads, model, products):
    return pl.CostEstimate(
        flops=heads * (products * 2 * length * length * 64 + 2 * length * model * 256) // SHARE,
        bytes_accessed=4 * length * model * 2 // SHARE,
        transcendentals=heads * 2 * length * length // SHARE,
    )


def weight_specs(weights, start=0):
    return [
        pl.BlockSpec((w.shape[0], 1, w.shape[2], 256), lambda j: (0, j + start, 0, 0))
        for w in weights
    ]


def attention_call(flip, size, heads, x, cosines, sines, q_gain, k_gain, weights):
    members = len(x)
    own, model = x[0].shape[0], 128 * (x[0].shape[1] // 128 - 1)
    length = members * own
    return pl.pallas_call(
        functools.partial(attention_kernel, members, len(weights), size),
        grid=(heads,),
        in_specs=[smem()]
        + [single_spec((own, model))] * members
        + [single_spec(a.shape) for a in (cosines, sines, q_gain, k_gain)]
        + weight_specs(weights),
        out_specs=[pl.BlockSpec((own, 128), lambda j: (0, j))] * members,
        out_shape=[jax.ShapeDtypeStruct((own, heads * 128), bf16)] * members,
        scratch_shapes=[
            pltpu.VMEM((model, 256), bf16),
            pltpu.VMEM((length, 256), f32),
            pltpu.VMEM((length, 128), bf16),
            pltpu.VMEM((length, 64), bf16),
            pltpu.VMEM((64, length), bf16),
            pltpu.VMEM((length, 128), bf16),
        ],
        compiler_params=pltpu.CompilerParams(vmem_limit_bytes=48 * 2**20),
        cost_estimate=attention_cost(length, heads, model, 4),
        name="attention",
    )(flip, *x, cosines, sines, q_gain, k_gain, *weights)


def attention_back_call(
    flip, size, start, heads, x, x_t, d_attn_t, mixed, cosines, sines, q_gain, k_gain, d_mixed, weights
):
    members = len(x)
    own, model = x_t[0].shape[1], x_t[0].shape[0]
    length = members * own
    slots, heights = grad_slots(model)
    eighth = model // 8
    return pl.pallas_call(
        functools.partial(attention_back_kernel, members, len(weights), slots, heads, size),
        grid=(heads,),
        in_specs=[smem()]
        + [single_spec(s) for s in [(own, model)] * members + [(model, own)] * (2 * members)]
        + [pl.BlockSpec((own, 128), lambda j: (0, j + start))] * members
        + [single_spec(a.shape) for a in (cosines, sines, q_gain, k_gain)]
        + [pl.BlockSpec((own, 128), lambda j: (0, j + start))] * members
        + weight_specs(weights, start),
        out_specs=[single_spec((own, model))] * members
        + [whole_spec((2, 128))]
        + [pl.BlockSpec((1, n * eighth, 384), lambda j: (j, 0, 0)) for n in heights],
        out_shape=[jax.ShapeDtypeStruct((own, model), bf16)] * members
        + [jax.ShapeDtypeStruct((2, 128), f32)]
        + [jax.ShapeDtypeStruct((heads, n * eighth, 384), bf16) for n in heights],
        scratch_shapes=[
            pltpu.VMEM((model, 256), bf16),
            pltpu.VMEM((length, 256), f32),
            pltpu.VMEM((length, 128), bf16),
            pltpu.VMEM((length, 64), bf16),
            pltpu.VMEM((length, 64), bf16),
            pltpu.VMEM((64, length), bf16),
            pltpu.VMEM((length, 128), bf16),
            pltpu.VMEM((length, 128), f32),
            pltpu.VMEM((length, 128), f32),
            pltpu.VMEM((length, 256), bf16),
            pltpu.VMEM((length, 256), bf16),
            pltpu.VMEM((length, model), f32),
        ],
        compiler_params=pltpu.CompilerParams(vmem_limit_bytes=58 * 2**20),
        cost_estimate=attention_cost(length, heads, model, 10),
        name="attention_back",
    )(flip, *x, *x_t, *d_attn_t, *mixed, cosines, sines, q_gain, k_gain, *d_mixed, *weights)


def local(
    tokens,
    positions,
    cotangent,
    q_weight,
    key_matrix,
    value_matrix,
    out_weight,
    gate_weight,
    up_weight,
    down_weight,
    attn_gain,
    ffn_gain,
    q_gain,
    k_gain,
):
    model = tokens.shape[2]
    rows_here = q_weight.shape[0]
    members = 2 * lax.axis_size("s")
    q_cols, kv_cols = q_weight.shape[1], key_matrix.shape[1]
    heads = kv_cols // 64 // members
    chunks = len(CHUNKS)
    core = lax.axis_index("c")
    first_member = 2 * lax.axis_index("s")
    members_at = jnp.stack([first_member + core, first_member + 1 - core]).astype(jnp.int32)
    flip = jnp.stack([flip_at(), chip_at()]).astype(jnp.int32)

    attn_mine, attn_away = pack_call(
        functools.partial(pack_attn_kernel, heads),
        members_at,
        (heads + heads // 2, rows_here, 256),
        (q_weight, key_matrix, value_matrix, out_weight),
    )
    attn_own = core_pair(attn_mine, swap_core(attn_away), 256, 0, 1)
    attn_gather = Gather(attn_own)
    attn_blocks = attn_gather.blocks()
    ffn_cols = gate_weight.shape[1] // members
    tile = ffn_cols // sum(CHUNKS)
    ffn_mine, ffn_away = pack_call(
        pack_ffn_kernel, members_at, (3, rows_here, ffn_cols), (gate_weight, up_weight, down_weight)
    )
    ffn_other = swap_core(ffn_away)
    gathers = []
    for k, count in enumerate(CHUNKS):
        own_part = core_pair(ffn_mine, ffn_other, tile, sum(CHUNKS[:k]), count)
        before = (gathers[-1] if k else attn_gather).first
        gathers.append(Gather(own_part, *before))

    high, low = positions // 128, positions % 128
    place_cols = jnp.stack([high, low], axis=2).astype(bf16)
    place_cols = jnp.pad(place_cols, ((0, 0), (0, 0), (0, 126)))
    tok = to_sequence(tokens, place_cols)
    quarters, size, _ = tok.shape
    own = quarters * size
    length = own * members
    tok = tok.reshape(own, model + 128)
    place_cols = tok[:, model:]
    tok = tok[:, :model].astype(f32)
    attn_gain_r = relative(attn_gain)
    ffn_gain_r = relative(ffn_gain)
    in_scale = rms_scale(tok)
    in_hat = tok * in_scale
    x = group_gather(jnp.concatenate([(in_hat * attn_gain_r).astype(bf16), place_cols], axis=1))
    x_t = [turn(a, model) for a in x]

    pos = [a[:, model : model + 2].astype(f32) for a in x]
    pos = jnp.stack([(p[:, 0] * 128.0 + p[:, 1]).reshape(quarters, size) for p in pos], axis=1)
    if pair_group():
        pos = jnp.where(core == 0, pos, pos[:, ::-1])
    inverse = rope_base ** (-(2.0 * jnp.arange(32, dtype=f32)) / 64)
    turned = pos.reshape(length)[:, None] * inverse[None, :]
    cosines = jnp.tile(jnp.cos(turned), (1, 4))
    sines = jnp.tile(jnp.sin(turned), (1, 4))
    q_gain2 = jnp.tile(q_gain, 2)[None]
    k_gain2 = jnp.tile(k_gain, 2)[None]

    cot_own = to_sequence(after(cotangent, x[0])).reshape(own, model)
    cot = group_gather(cot_own)
    cot_t = [turn(a, model) for a in cot]

    mixed = attention_call(
        after(flip, *gathers[0].first), size, heads, x, cosines, sines, q_gain2, k_gain2, attn_blocks
    )
    out_w = jnp.concatenate(
        [
            jnp.concatenate([b[i, heads + j] for j in range(heads // 2)], axis=1)
            for b in attn_blocks
            for i in range(b.shape[0])
        ],
        axis=0,
    )
    mixed = [after(mixed[0], *gathers[0].second, cot[1]), *mixed[1:]]
    residual = tok + group_scatter([[dot(m, out_w, NT) for m in mixed]])
    residual = after(residual, *gathers[1].first)
    mid_scale = rms_scale(residual)
    mid_hat = residual * mid_scale
    mid = group_gather((mid_hat * ffn_gain_r).astype(bf16))
    mid_t = [turn(a, model) for a in mid]

    out_parts, mid_parts, sums = [], [], []

    def step_all(*which):
        return [a for i in which for a in sums[i].advance()]

    for k in range(chunks):
        waits = []
        if k == 0:
            waits = gathers[1].second
        elif k == 1:
            waits = gathers[2].first
        else:
            waits = step_all(0)
        parts = ffn_call(
            tile,
            CHUNKS[k],
            [after(mid[0], *waits), *mid[1:]],
            mid_t,
            cot,
            cot_t,
            gathers[k].blocks(),
        )
        out_parts.append(parts[:members])
        mid_parts.append(parts[members : 2 * members])
        sums.append(Reduction(parts[2 * members :]))

    d_mid = group_scatter(mid_parts)
    ffn_gain_part = jnp.sum(d_mid * mid_hat, axis=0)
    d_resid = cot_own.astype(f32) + norm_back(d_mid, mid_hat, mid_scale, ffn_gain_r)
    d_attn = group_gather(d_resid.astype(bf16))
    waits = step_all(0, 1) + step_all(0, 1)
    d_mixed = [dot(d, out_w).astype(bf16) for d in d_attn]
    d_attn_t = [turn(d, model) for d in d_attn]

    calls = 2 if heads % 4 == 0 else 1
    d_in_parts, gain_parts = [], []
    for call in range(calls):
        waits = waits + step_all(2) if call == 0 else step_all(0, 1, 2) + step_all(2)
        parts = attention_back_call(
            after(flip, *waits),
            size,
            call * (heads // calls),
            heads // calls,
            x,
            x_t,
            d_attn_t,
            mixed,
            cosines,
            sines,
            q_gain2,
            k_gain2,
            d_mixed,
            attn_blocks,
        )
        d_in_parts.append(parts[:members])
        gain_parts.append(parts[members])
        sums.append(Reduction(parts[members + 1 :]))
    head_gains = sum(gain_parts)
    d_in_parts[-1] = [after(d_in_parts[-1][0], *step_all(1, 2)), *d_in_parts[-1][1:]]
    out_parts[0] = [after(out_parts[0][0], d_in_parts[0][0]), *out_parts[0][1:]]
    while any(r.step < 5 for r in sums):
        step_all(*[i for i, r in enumerate(sums) if r.step < 5])
    ffn_sums = [r.state for r in sums[:chunks]]
    heads_sums = [r.state for r in sums[chunks:]]
    d_in = group_scatter(d_in_parts)
    attn_gain_part = jnp.sum(d_in * in_hat, axis=0)
    input_grad = d_resid + norm_back(d_in, in_hat, in_scale, attn_gain_r)
    input_grad = from_sequence(input_grad.astype(bf16).reshape(quarters, size, model))

    output = (residual + group_scatter(out_parts)).astype(bf16)
    output = from_sequence(output.reshape(quarters, size, model))

    gain_sums = sum_all(
        jnp.concatenate(
            [
                relative(attn_gain_part),
                relative(ffn_gain_part),
                head_gains[0, :64] + head_gains[0, 64:],
                head_gains[1, :64],
            ]
        ),
        ffn_sums[-1][0],
    )

    if members == 2:
        ffn_grads = finish_ffn_call(ffn_sums)
        q_grad, k_grad, v_grad, out_grad = finish_heads_call(heads_sums)
    else:
        heads_all = [every_member(h) for h in heads_sums]
        every = jnp.concatenate([h[i] for i in range(members) for h in heads_all], axis=0)
        every = every.transpose(1, 0, 2).astype(f32)
        ffn_sums = [every_member(s) for s in ffn_sums]
        q_grad = every[:, :, :128].reshape(rows_here, q_cols)
        k_grad = every[:, :, 128:192].reshape(rows_here, kv_cols)
        v_grad = every[:, :, 192:256].reshape(rows_here, kv_cols)
        out_grad = every[:, :, 256:].reshape(rows_here, q_cols)
        ffn_grads = [
            jnp.concatenate(
                [ffn_sums[k][i][w] for i in range(members) for k in range(chunks)], axis=1
            ).astype(f32)
            for w in range(3)
        ]
    return (
        output,
        input_grad,
        q_grad,
        k_grad,
        v_grad,
        out_grad,
        ffn_grads[0],
        ffn_grads[1],
        ffn_grads[2],
        gain_sums[:model],
        gain_sums[model : 2 * model],
        gain_sums[2 * model : 2 * model + 64],
        gain_sums[2 * model + 64 :],
    )


def solution(mesh):
    dp, seq = mesh.devices.shape
    lines = 4
    fine = Mesh(mesh.devices.reshape(dp // 4, 2, 2, lines, seq // lines), EVERY)
    rows, cols = ("o", "x", "c"), ("z", "s")
    tokens = P(rows, cols, None)
    weight = P(rows, None)
    return jax.shard_map(
        local,
        mesh=fine,
        in_specs=(tokens, P(rows, cols), tokens) + (weight,) * 7 + (P(),) * 4,
        out_specs=(tokens, tokens) + (weight,) * 7 + (P(),) * 4,
        check_vma=False,
    )
```

```python
import functools

import jax
import jax.numpy as jnp
from jax import lax
from jax.experimental import pallas as pl
from jax.experimental.pallas import tpu as pltpu
from jax.sharding import Mesh, PartitionSpec as P

epsilon = 1e-05
rope_base = 1000000.0
f32 = jnp.float32
bf16 = jnp.bfloat16
SWAP = ((0, 1), (1, 0))
EVERY = ("o", "x", "c", "z", "s")
NT = (((1,), (1,)), ((), ()))
NN = (((1,), (0,)), ((), ()))


def dot(left, right, dims=NN):
    return lax.dot_general(left, right, dims, preferred_element_type=f32)


def rms_scale(rows):
    return lax.rsqrt(jnp.mean(rows * rows, axis=-1, keepdims=True) + epsilon)


def norm_back(grad_out, normed_hat, inv_scale, gain):
    scaled = grad_out * gain
    return inv_scale * (scaled - normed_hat * jnp.mean(scaled * normed_hat, axis=-1, keepdims=True))


def square():
    return lax.axis_size("o") == 2 and lax.axis_size("x") == 2


def pair_group():
    return lax.axis_size("s") == 1


def chip_at():
    if not square():
        return jnp.int32(0)
    return 2 * lax.axis_index("o") + lax.axis_index("x")


def flip_at():
    return lax.axis_index("c") if pair_group() else jnp.int32(0)


def relative(vector):
    if not square():
        return vector
    quarter = vector.shape[0] // 4
    blocks = [
        lax.dynamic_slice_in_dim(vector, (chip_at() ^ i) * quarter, quarter) for i in range(4)
    ]
    return jnp.concatenate(blocks)


def after(array, *others):
    return lax.optimization_barrier((array, *others))[0]


def swap_core(array):
    return lax.ppermute(array, "c", SWAP)


def group_gather(rows):
    if pair_group():
        return [rows, swap_core(rows)]
    full = lax.all_gather(rows, ("s", "c"), axis=0)
    return [full[i] for i in range(full.shape[0])]


def group_scatter(parts):
    if pair_group():
        away = sum(p[1].astype(f32) for p in parts).astype(bf16)
        return sum(p[0].astype(f32) for p in parts) + swap_core(away).astype(f32)
    total = jnp.stack([sum(p[m].astype(f32) for p in parts) for m in range(len(parts[0]))])
    return lax.psum_scatter(total, ("s", "c"), scatter_dimension=0, tiled=False)


def merge_kernel(relate, at_ref, mine_ref, other_ref, out_ref):
    core, chip = at_ref[0], at_ref[1]
    if not relate:
        out_ref[:, core] = mine_ref[...]
        out_ref[:, 1 - core] = other_ref[...]
        return
    quarter = mine_ref.shape[-1] // 4
    for r in range(4):
        to = pl.ds(pl.multiple_of((chip ^ r) * quarter, quarter), quarter)
        at = slice(r * quarter, (r + 1) * quarter)
        out_ref[:, core, :, to] = mine_ref[:, :, at]
        out_ref[:, 1 - core, :, to] = other_ref[:, :, at]


def smem():
    return pl.BlockSpec(memory_space=pltpu.SMEM)


def place():
    return jnp.stack([lax.axis_index("c"), chip_at()]).astype(jnp.int32)


def small_cost(bytes_moved):
    return pl.CostEstimate(flops=0, bytes_accessed=bytes_moved, transcendentals=0)


def by_core(mine, other, relate=False):
    n, rows, width = mine.shape
    step = 1 if n % 3 else n // 3
    block = pl.BlockSpec((step, rows, width), lambda i: (i, 0, 0))
    out = pl.pallas_call(
        functools.partial(merge_kernel, relate),
        grid=(n // step,),
        in_specs=[smem(), block, block],
        out_specs=pl.BlockSpec((step, 2, rows, width), lambda i: (i, 0, 0, 0)),
        out_shape=jax.ShapeDtypeStruct((n, 2, rows, width), mine.dtype),
        cost_estimate=small_cost(mine.size * 8),
        compiler_params=pltpu.CompilerParams(vmem_limit_bytes=32 * 2**20),
        name="merge",
    )(place(), mine, other)
    return out.reshape(n, 2 * rows, width)


def enter_kernel(at_ref, rows_ref, *refs):
    core, chip = at_ref[0], at_ref[1]
    mine_ref, away_ref = refs[-2:]
    size = mine_ref.shape[1]
    model = rows_ref.shape[-1]
    quarter = model // 4
    for ref, which in ((mine_ref, core), (away_ref, 1 - core)):
        span = pl.ds(pl.multiple_of(which * size, size), size)
        for r in range(4):
            at = pl.ds(pl.multiple_of((chip ^ r) * quarter, quarter), quarter)
            ref[:, :, r * quarter : (r + 1) * quarter] = rows_ref[:, span, at]
        if len(refs) == 3:
            ref[:, :, model:] = refs[0][:, span, :]


def to_sequence(rows, *extra):
    seqs, count, width = rows.shape
    width += sum(e.shape[2] for e in extra)
    half = jax.ShapeDtypeStruct((seqs, count // 2, width), rows.dtype)
    mine, away = pl.pallas_call(
        enter_kernel,
        in_specs=[smem()] + [pl.BlockSpec(memory_space=pltpu.VMEM)] * (1 + len(extra)),
        out_specs=[pl.BlockSpec(memory_space=pltpu.VMEM)] * 2,
        out_shape=[half, half],
        cost_estimate=small_cost(rows.size * 4),
        name="enter",
    )(place(), rows, *extra)
    other = swap_core(away)
    every = by_core(mine.reshape(1, -1, width), other.reshape(1, -1, width))
    return lax.all_to_all(every.reshape(2 * seqs, count // 2, width), "z", 0, 0, tiled=True)


def from_sequence(rows):
    core = lax.axis_index("c")
    every = lax.all_to_all(rows, "z", 0, 0, tiled=True)
    seqs = every.shape[0] // 2
    away = lax.dynamic_slice_in_dim(every, (1 - core) * seqs, seqs)
    mine = lax.dynamic_slice_in_dim(every, core * seqs, seqs)
    return by_core(mine, swap_core(away), relate=True)


def pair_kernel(at_ref, mine_ref, other_ref, out_ref):
    core = at_ref[0]
    out_ref[core] = mine_ref[...]
    out_ref[1 - core] = other_ref[...]


def core_pair(mine, other, tile, start, count):
    n, rows, _ = mine.shape
    block = pl.BlockSpec((n, rows, tile), lambda i: (0, 0, start + i))
    return pl.pallas_call(
        pair_kernel,
        grid=(count,),
        in_specs=[smem(), block, block],
        out_specs=pl.BlockSpec((2, n, rows, tile), lambda i: (0, 0, 0, i)),
        out_shape=jax.ShapeDtypeStruct((2, n, rows, count * tile), mine.dtype),
        cost_estimate=small_cost(8 * n * rows * count * tile),
        name="core_pair",
    )(place(), mine, other)


class Gather:
    def __init__(self, own, *before):
        self.own = own
        if square():
            own = after(own, *before)
            self.first = [lax.ppermute(own, "x", SWAP), lax.ppermute(own, "o", SWAP)]
            by_x, by_o = self.first
            self.second = [
                lax.ppermute(by_x[:1], "o", SWAP),
                lax.ppermute(by_o[1:], "x", SWAP),
            ]
        else:
            self.first = self.second = []

    def blocks(self):
        if square():
            return [self.own, *self.first, *self.second]
        full = lax.all_gather(self.own, ("o", "x"), axis=0, tiled=True)
        return [full[i : i + 2] for i in range(0, full.shape[0], 2)]


def grad_slots(model):
    if square():
        return [(2, 0), (3, 0), (0, 0), (3, 1), (2, 1), (1, 0), (0, 1), (1, 1)], [2, 2, 2, 2]
    return [(0, i) for i in range(8)], [8]


def put_rows(out_refs, slots, index, cols, term):
    size = term.shape[0] // 8
    for part, (which, row) in enumerate(slots):
        out_refs[which][index, row * size : (row + 1) * size, cols] = term[
            part * size : (part + 1) * size
        ].astype(bf16)


def add_up(*terms):
    return functools.reduce(jnp.add, [t.astype(f32) for t in terms]).astype(bf16)


def combine_kernel(keep_a, come_a, last_a, keep_b, come_b, last_b, out_ref):
    half = last_a.shape[1]
    for at, (keep, come, last) in enumerate(((keep_a, come_a, last_a), (keep_b, come_b, last_b))):
        out_ref[:, at * half : (at + 1) * half, :] = add_up(keep[...], come[...], last[...])


def combine(keep_a, come_a, last_a, keep_b, come_b, last_b):
    n, half, width = last_a.shape
    block = pl.BlockSpec((1, half, width), lambda i: (i, 0, 0))
    return pl.pallas_call(
        combine_kernel,
        grid=(n,),
        in_specs=[block] * 6,
        out_specs=pl.BlockSpec((1, 2 * half, width), lambda i: (i, 0, 0)),
        out_shape=jax.ShapeDtypeStruct((n, 2 * half, width), bf16),
        cost_estimate=small_cost(16 * n * half * width),
        name="combine",
    )(keep_a, come_a, last_a, keep_b, come_b, last_b)


class Reduction:
    def __init__(self, outs):
        self.step = 0
        self.state = outs
        if square():
            self.state = [
                *outs,
                lax.ppermute(outs[0], "x", SWAP),
                lax.ppermute(outs[1], "o", SWAP),
            ]

    def advance(self):
        step, self.step = self.step, self.step + 1
        state = self.state
        on_line = lax.axis_size("z") == 4
        if step == 0 and square():
            _, _, keep_a, keep_b, come_a, come_b = state
            half = keep_a.shape[1] // 2
            go_a = add_up(keep_a[:, half:], come_a[:, half:])
            go_b = add_up(keep_b[:, half:], come_b[:, half:])
            last_a, last_b = lax.ppermute(go_a, "o", SWAP), lax.ppermute(go_b, "x", SWAP)
            self.state = (keep_a, come_a, last_a, keep_b, come_b, last_b)
            return [go_a, go_b]
        if step == 1:
            if square():
                here = combine(*state)
            else:
                here = lax.psum_scatter(
                    state[0].astype(f32), ("o", "x"), scatter_dimension=1, tiled=True
                ).astype(bf16)
            come = lax.ppermute(here, "z", ((0, 1), (3, 2))) if on_line else None
            self.state = (here, come)
            return [here]
        if step == 2 and on_line:
            here = add_up(*state)
            self.state = (here, lax.ppermute(here, "z", ((1, 2), (2, 1))))
            return [here]
        if step == 3 and on_line:
            here = add_up(*state)
            self.state = (here, lax.ppermute(here, "z", ((1, 0), (2, 3))))
            return [here]
        if step == 4:
            if on_line:
                at = lax.axis_index("z")
                total = jnp.where((at == 0) | (at == 3), state[1], state[0])
            else:
                total = lax.psum(state[0].astype(f32), "z").astype(bf16)
            core = lax.axis_index("c")
            half = total.shape[1] // 2
            mine = lax.dynamic_slice_in_dim(total, core * half, half, 1)
            away = lax.dynamic_slice_in_dim(total, (1 - core) * half, half, 1)
            self.state = (mine, swap_core(away))
            return [total]
        return []


def every_member(done):
    mine, other = done
    first = lax.axis_index("c") == 0
    pair = jnp.stack([jnp.where(first, mine, other), jnp.where(first, other, mine)])
    every = lax.all_gather(pair, "s", axis=0, tiled=True)
    return [every[i] for i in range(every.shape[0])]


def sum_all(terms, before):
    if not (square() and pair_group() and lax.axis_size("z") == 4):
        return lax.psum(terms, EVERY)
    for axis, perm in (
        ("c", SWAP),
        ("x", SWAP),
        ("o", SWAP),
        ("z", ((0, 1), (1, 0), (2, 3), (3, 2))),
        ("z", ((0, 2), (2, 0), (1, 3), (3, 1))),
    ):
        if axis == "z":
            terms = after(terms, before)
        terms = terms + lax.ppermute(terms, axis, perm)
    return terms


def member_cols(start, count):
    return pl.ds(pl.multiple_of(start, 128), count)


def pack_attn_kernel(heads, at_ref, q_ref, k_ref, v_ref, o_ref, *outs):
    for i in range(2):
        member, attn_ref = at_ref[i], outs[i]
        for j in range(0, heads, 2):
            head = member * heads + j
            keys = k_ref[:, member_cols(head * 64, 128)]
            values = v_ref[:, member_cols(head * 64, 128)]
            for m in range(2):
                attn_ref[j + m, :, :128] = q_ref[:, member_cols((head + m) * 128, 128)]
                attn_ref[j + m, :, 128:192] = keys[:, m * 64 : (m + 1) * 64]
                attn_ref[j + m, :, 192:] = values[:, m * 64 : (m + 1) * 64]
        for j in range(heads // 2):
            attn_ref[heads + j] = o_ref[:, member_cols(member * heads * 128 + j * 256, 256)]


def pack_ffn_kernel(at_ref, g_ref, u_ref, d_ref, *outs):
    for i in range(2):
        width = outs[i].shape[2]
        for w, ref in enumerate((g_ref, u_ref, d_ref)):
            outs[i][w] = ref[:, member_cols(at_ref[i] * width, width)]


def pack_call(kernel, members_at, out, weights):
    return pl.pallas_call(
        kernel,
        in_specs=[smem()] + [pl.BlockSpec(memory_space=pltpu.VMEM)] * len(weights),
        out_specs=[pl.BlockSpec(memory_space=pltpu.VMEM)] * 2,
        out_shape=[jax.ShapeDtypeStruct(out, bf16)] * 2,
        cost_estimate=small_cost(2 * 4 * out[0] * out[1] * out[2]),
        compiler_params=pltpu.CompilerParams(vmem_limit_bytes=32 * 2**20),
        name="pack",
    )(members_at, *weights)


def finish_ffn_kernel(at_ref, *refs):
    mines, others, outs = refs[:-3:2], refs[1:-3:2], refs[-3:]
    first = at_ref[0] == 0
    total = sum(m.shape[2] for m in mines)
    start = 0
    for mine_ref, other_ref in zip(mines, others):
        width = mine_ref.shape[2]
        mine, other = mine_ref[0], other_ref[0]
        low = jnp.where(first, mine, other).astype(f32)
        high = jnp.where(first, other, mine).astype(f32)
        for w in range(3):

            @pl.when(pl.program_id(0) == w)
            def _():
                outs[w][:, start : start + width] = low
                outs[w][:, total + start : total + start + width] = high

        start += width


def finish_ffn_call(sums):
    rows = sums[0][0].shape[1]
    out = jax.ShapeDtypeStruct((rows, 2 * sum(s[0].shape[2] for s in sums)), f32)
    arrays = [a for s in sums for a in s]
    return pl.pallas_call(
        finish_ffn_kernel,
        grid=(3,),
        in_specs=[smem()] + [pl.BlockSpec((1, *a.shape[1:]), lambda w: (w, 0, 0)) for a in arrays],
        out_specs=[whole_spec(out.shape)] * 3,
        out_shape=[out] * 3,
        cost_estimate=small_cost(out.size * 18),
        compiler_params=pltpu.CompilerParams(vmem_limit_bytes=40 * 2**20),
        name="finish_ffn",
    )(place(), *arrays)


def finish_heads_kernel(calls, at_ref, *refs):
    first = at_ref[0] == 0
    q_ref, k_ref, v_ref, o_ref = refs[2 * calls :]
    per_call = refs[0].shape[0]
    heads = calls * per_call

    def pick(head):
        mine, other = refs[2 * (head // per_call)], refs[2 * (head // per_call) + 1]
        mine, other = mine[head % per_call], other[head % per_call]
        return [
            jnp.where(first, mine, other).astype(f32),
            jnp.where(first, other, mine).astype(f32),
        ]

    for j in range(0, heads, 2):
        pairs = [pick(j), pick(j + 1)]
        for g in range(2):
            pair = [p[g] for p in pairs]
            head = g * heads + j
            for m in range(2):
                at = slice((head + m) * 128, (head + m + 1) * 128)
                q_ref[:, at] = pair[m][:, :128]
                o_ref[:, at] = pair[m][:, 256:]
            at = slice(head * 64, (head + 2) * 64)
            k_ref[:, at] = jnp.concatenate([p[:, 128:192] for p in pair], axis=1)
            v_ref[:, at] = jnp.concatenate([p[:, 192:256] for p in pair], axis=1)


def finish_heads_call(heads_sums):
    per_call, rows, _ = heads_sums[0][0].shape
    heads = per_call * len(heads_sums)
    wide = jax.ShapeDtypeStruct((rows, heads * 256), f32)
    narrow = jax.ShapeDtypeStruct((rows, heads * 128), f32)
    return pl.pallas_call(
        functools.partial(finish_heads_kernel, len(heads_sums)),
        in_specs=[smem()] + [pl.BlockSpec(memory_space=pltpu.VMEM)] * (2 * len(heads_sums)),
        out_specs=[pl.BlockSpec(memory_space=pltpu.VMEM)] * 4,
        out_shape=[wide, narrow, narrow, wide],
        cost_estimate=small_cost(rows * heads * 768 * 6),
        name="finish_heads",
    )(place(), *[a for s in heads_sums for a in s])


def fill(scratch, refs, index):
    row = 0
    for ref in refs:
        for part in range(ref.shape[0]):
            block = ref[part, index]
            scratch[row : row + block.shape[0], :] = block
            row += block.shape[0]


def ffn_kernel(members, blocks, slots, steps, *refs):
    xs, xts, cots, cotts = [refs[i * members : (i + 1) * members] for i in range(4)]
    rest = refs[4 * members :]
    weights, rest = rest[:blocks], rest[blocks:]
    out_refs, mid_refs = rest[:members], rest[members : 2 * members]
    grads = rest[2 * members : -8]
    gate, up, down, hid, dgate, dup, out_acc, mid_acc = rest[-8:]
    step = pl.program_id(0)
    for i, scratch in enumerate((gate, up, down)):
        fill(scratch, weights, i)

    @pl.when(step == 0)
    def _():
        out_acc[...] = jnp.zeros_like(out_acc)
        mid_acc[...] = jnp.zeros_like(mid_acc)

    own = xs[0].shape[0]
    rows = 512
    for m in range(members):

        def body(i, carry):
            at = pl.ds(pl.multiple_of(i * rows, rows), rows)
            to = pl.ds(pl.multiple_of(m * own + i * rows, rows), rows)
            x = xs[m][at, :]
            g = dot(x, gate[...])
            u = dot(x, up[...])
            dh = dot(cots[m][at, :], down[...])
            sig = jax.nn.sigmoid(g)
            act = g * sig
            h = (act * u).astype(bf16)
            dg = (dh * u * sig * (1.0 + g * (1.0 - sig))).astype(bf16)
            du = (dh * act).astype(bf16)
            hid[to, :] = h
            dgate[to, :] = dg
            dup[to, :] = du
            out_acc[to, :] += dot(h, down[...], NT)
            mid_acc[to, :] += dot(dg, gate[...], NT) + dot(du, up[...], NT)
            return carry

        lax.fori_loop(0, own // rows, body, 0)

    def over_rows(lefts, at, right):
        return functools.reduce(
            jnp.add,
            [dot(l[at, :], right[m * own : (m + 1) * own, :]) for m, l in enumerate(lefts)],
        )

    model = xts[0].shape[0]
    for i, (lefts, right) in enumerate(((xts, dgate), (xts, dup), (cotts, hid))):
        term = over_rows(lefts, slice(0, model), right)
        put_rows(grads, slots, i, slice(None), term)

    @pl.when(step == steps - 1)
    def _():
        for m in range(members):
            out_refs[m][...] = out_acc[m * own : (m + 1) * own, :].astype(bf16)
            mid_refs[m][...] = mid_acc[m * own : (m + 1) * own, :].astype(bf16)


def turn_kernel(in_ref, out_ref):
    out_ref[...] = in_ref[...].T


def turn(rows, width):
    count = rows.shape[0]
    return pl.pallas_call(
        turn_kernel,
        grid=(2,),
        in_specs=[pl.BlockSpec((count, width // 2), lambda i: (0, i))],
        out_specs=pl.BlockSpec((width // 2, count), lambda i: (i, 0)),
        out_shape=jax.ShapeDtypeStruct((width, count), rows.dtype),
        cost_estimate=small_cost(rows.size * 4),
        name="turn",
    )(rows)


def whole_spec(shape):
    zeros = (0,) * len(shape)
    return pl.BlockSpec(shape, lambda *_: zeros)


def single_spec(shape):
    zeros = (0,) * len(shape)
    return pl.BlockSpec(shape, lambda *_: zeros, pipeline_mode=pl.Buffered(1))


SHARE = 32

CHUNKS = (3, 3, 3)


def ffn_call(tile, steps, x, x_t, cot, cot_t, weights):
    members = len(x)
    own, model = x[0].shape
    rows = own * members
    width = steps * tile
    slots, heights = grad_slots(model)
    size = model // 8
    return pl.pallas_call(
        functools.partial(ffn_kernel, members, len(weights), slots, steps),
        grid=(steps,),
        in_specs=[single_spec((own, model))] * members
        + [single_spec(a.shape) for a in (*x_t, *cot, *cot_t)]
        + [
            pl.BlockSpec((w.shape[0], 3, w.shape[2], tile), lambda j: (0, 0, 0, j))
            for w in weights
        ],
        out_specs=[single_spec((own, model))] * (2 * members)
        + [pl.BlockSpec((3, n * size, tile), lambda j: (0, 0, j)) for n in heights],
        out_shape=[jax.ShapeDtypeStruct((own, model), bf16)] * (2 * members)
        + [jax.ShapeDtypeStruct((3, n * size, width), bf16) for n in heights],
        scratch_shapes=[pltpu.VMEM((model, tile), bf16)] * 3
        + [pltpu.VMEM((rows, tile), bf16)] * 3
        + [pltpu.VMEM((rows, model), f32)] * 2,
        compiler_params=pltpu.CompilerParams(vmem_limit_bytes=58 * 2**20),
        cost_estimate=pl.CostEstimate(
            flops=18 * rows * model * width // SHARE,
            bytes_accessed=(6 * rows * model * 2 + 12 * model * width) // SHARE,
            transcendentals=rows * width // SHARE,
        ),
        name="ffn",
    )(*x, *x_t, *cot, *cot_t, *weights)


def lanes_first():
    return lax.broadcasted_iota(jnp.int32, (1, 128), 1) < 64


def head_mean(square_terms):
    first = lanes_first()
    low = jnp.sum(jnp.where(first, square_terms, 0.0), axis=-1, keepdims=True)
    high = jnp.sum(jnp.where(first, 0.0, square_terms), axis=-1, keepdims=True)
    return jnp.where(first, low, high) * (1.0 / 64)


def partner(u):
    low = (lax.broadcasted_iota(jnp.int32, (1, 128), 1) & 63) < 32
    return jnp.where(low, -pltpu.roll(u, 96, 1), pltpu.roll(u, 32, 1))


def natural_rows(flip, members, own, size):
    for m in range(members):
        for i in range(own // size):
            to = pl.multiple_of((i * members + (m ^ flip)) * size, size)
            yield m, i * size, pl.ds(to, size)


def project(flip, size, xs, weights, w_scr, qkv):
    fill(w_scr, weights, 0)
    own = xs[0].shape[0]
    terms = [dot(x[...], w_scr[...]) for x in xs]
    for m, row, at in natural_rows(flip, len(xs), own, size):
        qkv[at, :] = terms[m][row : row + size]


def heads_of(u, gain, cosines, sines):
    inv = lax.rsqrt(head_mean(u * u) + epsilon)
    hat = u * inv
    turned = hat * gain
    return inv, hat, turned * cosines + partner(turned) * sines


def stack_heads(block):
    return jnp.concatenate([block[:, :64], block[:, 64:]], axis=0)


def unstack_heads(turned):
    half = turned.shape[1] // 2
    return jnp.concatenate([turned[:, :half], turned[:, half:]], axis=0).T


BLOCK = 256


def probs_of(q2, keys, block):
    parts = []
    for at in range(block + 1):
        parts.append(dot(keys[at * BLOCK : (at + 1) * BLOCK, :], q2, NT))
    key_at = lax.broadcasted_iota(jnp.int32, parts[-1].shape, 0)
    query_at = lax.broadcasted_iota(jnp.int32, parts[-1].shape, 1) & (BLOCK - 1)
    parts[-1] = jnp.where(key_at <= query_at, parts[-1], -1e30)
    top = functools.reduce(jnp.maximum, [jnp.max(p, axis=0, keepdims=True) for p in parts])
    parts = [jnp.exp(p - top) for p in parts]
    total = functools.reduce(jnp.add, [jnp.sum(p, axis=0, keepdims=True) for p in parts])
    inv = 1.0 / total
    return [p * inv for p in parts]


def attention_kernel(members, blocks, size, at_ref, *refs):
    xs, rest = refs[:members], refs[members:]
    cos_ref, sin_ref, qg_ref, kg_ref = rest[:4]
    weights, rest = rest[4 : 4 + blocks], rest[4 + blocks :]
    mixed_refs, rest = rest[:members], rest[members:]
    w_scr, qkv, q_scr, k_scr, vt_scr, mixed_scr = rest
    flip = at_ref[0]
    project(flip, size, xs, weights, w_scr, qkv)
    cosines, sines = cos_ref[...], sin_ref[...]
    _, _, q = heads_of(qkv[:, :128], qg_ref[...], cosines, sines)
    q_scr[...] = q.astype(bf16) * jnp.asarray(0.125, bf16)
    _, _, k = heads_of(qkv[:, 128:], kg_ref[...], cosines, sines)
    k_scr[...] = k[:, :64].astype(bf16)
    vt_scr[...] = qkv[:, 192:].astype(bf16).T
    for block in range(q_scr.shape[0] // BLOCK):
        at = slice(block * BLOCK, (block + 1) * BLOCK)
        q2 = stack_heads(q_scr[at, :])
        probs = probs_of(q2, k_scr, block)
        total = None
        for i, p in enumerate(probs):
            term = dot(vt_scr[:, i * BLOCK : (i + 1) * BLOCK], p.astype(bf16))
            total = term if total is None else total + term
        mixed_scr[at, :] = unstack_heads(total).astype(bf16)
    for m, row, at in natural_rows(flip, members, xs[0].shape[0], size):
        mixed_refs[m][row : row + size, :] = mixed_scr[at, :]


def attention_back_kernel(members, blocks, slots, steps, size, at_ref, *refs):
    xs, xts, das, mixes = [refs[i * members : (i + 1) * members] for i in range(4)]
    rest = refs[4 * members :]
    cos_ref, sin_ref, qg_ref, kg_ref = rest[:4]
    dms, rest = rest[4 : 4 + members], rest[4 + members :]
    weights, rest = rest[:blocks], rest[blocks:]
    din_refs, gains_ref, grads = rest[:members], rest[members], rest[members + 1 : -12]
    rest = rest[-12:]
    w_scr, qkv, q_scr, k_scr, v_scr, kt_scr, dm_scr, dq_scr, dkv_scr, dall, dqkv, din_acc = rest
    flip = at_ref[0]
    own = xs[0].shape[0]
    step = pl.program_id(0)
    project(flip, size, xs, weights, w_scr, qkv)
    for m, row, at in natural_rows(flip, members, own, size):
        dm_scr[at, :] = dms[m][row : row + size, :]
    cosines, sines = cos_ref[...], sin_ref[...]
    q_gain, k_gain = qg_ref[...], kg_ref[...]
    q_inv, q_hat, q = heads_of(qkv[:, :128], q_gain, cosines, sines)
    q_scr[...] = q.astype(bf16) * jnp.asarray(0.125, bf16)
    k_inv, k_hat, k = heads_of(qkv[:, 128:], k_gain, cosines, sines)
    k_scr[...] = k[:, :64].astype(bf16)
    kt_scr[...] = k[:, :64].astype(bf16).T
    v_scr[...] = qkv[:, 192:].astype(bf16)
    dkv_scr[...] = jnp.zeros_like(dkv_scr)
    for block in range(q_scr.shape[0] // BLOCK):
        at = slice(block * BLOCK, (block + 1) * BLOCK)
        q2 = stack_heads(q_scr[at, :])
        do2 = stack_heads(dm_scr[at, :])
        probs = probs_of(q2, k_scr, block)
        backs = [
            dot(v_scr[i * BLOCK : (i + 1) * BLOCK, :], do2, NT) for i in range(block + 1)
        ]
        delta = functools.reduce(
            jnp.add, [jnp.sum(p * b, axis=0, keepdims=True) for p, b in zip(probs, backs)]
        )
        total = None
        for i, (p, b) in enumerate(zip(probs, backs)):
            ds = (p * (b - delta)).astype(bf16)
            keys = slice(i * BLOCK, (i + 1) * BLOCK)
            term = dot(kt_scr[:, keys], ds)
            total = term if total is None else total + term
            dkv_scr[keys, :] += jnp.concatenate([dot(ds, q2), dot(p.astype(bf16), do2)], axis=1)
        dq_scr[at, :] = unstack_heads(total) * 0.125
    first = lanes_first()
    dq = dq_scr[...].astype(bf16).astype(f32)
    dkv = dkv_scr[...].astype(bf16).astype(f32)
    dq = dq * cosines - partner(dq) * sines
    dk = dkv * cosines - partner(dkv) * sines
    q_part = jnp.sum(dq * q_hat, axis=0, keepdims=True)
    k_part = jnp.sum(jnp.where(first, dk * k_hat, 0.0), axis=0, keepdims=True)
    both = jnp.concatenate([q_part, k_part], axis=0)

    @pl.when(step == 0)
    def _():
        gains_ref[...] = both
        din_acc[...] = jnp.zeros_like(din_acc)

    @pl.when(step > 0)
    def _():
        gains_ref[...] += both

    scaled = dq * q_gain
    d_q = q_inv * (scaled - q_hat * head_mean(scaled * q_hat))
    scaled = dk * k_gain
    d_k = k_inv * (scaled - k_hat * head_mean(scaled * k_hat))
    dall[:, :128] = d_q.astype(bf16)
    dall[:, 128:] = jnp.where(first, d_k, dkv).astype(bf16)
    for m, row, at in natural_rows(flip, members, own, size):
        dqkv[m * own + row : m * own + row + size, :] = dall[at, :]
    din_acc[...] += dot(dqkv[...], w_scr[...], NT)
    term = sum(dot(xt[...], dqkv[m * own : (m + 1) * own, :]) for m, xt in enumerate(xts))
    put_rows(grads, slots, 0, slice(0, 256), term)
    term = sum(dot(da[...], mix[...]) for da, mix in zip(das, mixes))
    put_rows(grads, slots, 0, slice(256, 384), term)

    @pl.when(step == steps - 1)
    def _():
        for m in range(members):
            din_refs[m][...] = din_acc[m * own : (m + 1) * own, :].astype(bf16)


def attention_cost(length, heads, model, products):
    return pl.CostEstimate(
        flops=heads * (products * 2 * length * length * 64 + 2 * length * model * 256) // SHARE,
        bytes_accessed=4 * length * model * 2 // SHARE,
        transcendentals=heads * 2 * length * length // SHARE,
    )


def weight_specs(weights, start=0):
    return [
        pl.BlockSpec((w.shape[0], 1, w.shape[2], 256), lambda j: (0, j + start, 0, 0))
        for w in weights
    ]


def attention_call(flip, size, heads, x, cosines, sines, q_gain, k_gain, weights):
    members = len(x)
    own, model = x[0].shape[0], 128 * (x[0].shape[1] // 128 - 1)
    length = members * own
    return pl.pallas_call(
        functools.partial(attention_kernel, members, len(weights), size),
        grid=(heads,),
        in_specs=[smem()]
        + [single_spec((own, model))] * members
        + [single_spec(a.shape) for a in (cosines, sines, q_gain, k_gain)]
        + weight_specs(weights),
        out_specs=[pl.BlockSpec((own, 128), lambda j: (0, j))] * members,
        out_shape=[jax.ShapeDtypeStruct((own, heads * 128), bf16)] * members,
        scratch_shapes=[
            pltpu.VMEM((model, 256), bf16),
            pltpu.VMEM((length, 256), f32),
            pltpu.VMEM((length, 128), bf16),
            pltpu.VMEM((length, 64), bf16),
            pltpu.VMEM((64, length), bf16),
            pltpu.VMEM((length, 128), bf16),
        ],
        compiler_params=pltpu.CompilerParams(vmem_limit_bytes=48 * 2**20),
        cost_estimate=attention_cost(length, heads, model, 4),
        name="attention",
    )(flip, *x, cosines, sines, q_gain, k_gain, *weights)


def attention_back_call(
    flip, size, start, heads, x, x_t, d_attn_t, mixed, cosines, sines, q_gain, k_gain, d_mixed, weights
):
    members = len(x)
    own, model = x_t[0].shape[1], x_t[0].shape[0]
    length = members * own
    slots, heights = grad_slots(model)
    eighth = model // 8
    return pl.pallas_call(
        functools.partial(attention_back_kernel, members, len(weights), slots, heads, size),
        grid=(heads,),
        in_specs=[smem()]
        + [single_spec(s) for s in [(own, model)] * members + [(model, own)] * (2 * members)]
        + [pl.BlockSpec((own, 128), lambda j: (0, j + start))] * members
        + [single_spec(a.shape) for a in (cosines, sines, q_gain, k_gain)]
        + [pl.BlockSpec((own, 128), lambda j: (0, j + start))] * members
        + weight_specs(weights, start),
        out_specs=[single_spec((own, model))] * members
        + [whole_spec((2, 128))]
        + [pl.BlockSpec((1, n * eighth, 384), lambda j: (j, 0, 0)) for n in heights],
        out_shape=[jax.ShapeDtypeStruct((own, model), bf16)] * members
        + [jax.ShapeDtypeStruct((2, 128), f32)]
        + [jax.ShapeDtypeStruct((heads, n * eighth, 384), bf16) for n in heights],
        scratch_shapes=[
            pltpu.VMEM((model, 256), bf16),
            pltpu.VMEM((length, 256), f32),
            pltpu.VMEM((length, 128), bf16),
            pltpu.VMEM((length, 64), bf16),
            pltpu.VMEM((length, 64), bf16),
            pltpu.VMEM((64, length), bf16),
            pltpu.VMEM((length, 128), bf16),
            pltpu.VMEM((length, 128), f32),
            pltpu.VMEM((length, 128), f32),
            pltpu.VMEM((length, 256), bf16),
            pltpu.VMEM((length, 256), bf16),
            pltpu.VMEM((length, model), f32),
        ],
        compiler_params=pltpu.CompilerParams(vmem_limit_bytes=58 * 2**20),
        cost_estimate=attention_cost(length, heads, model, 10),
        name="attention_back",
    )(flip, *x, *x_t, *d_attn_t, *mixed, cosines, sines, q_gain, k_gain, *d_mixed, *weights)


def local(
    tokens,
    positions,
    cotangent,
    q_weight,
    key_matrix,
    value_matrix,
    out_weight,
    gate_weight,
    up_weight,
    down_weight,
    attn_gain,
    ffn_gain,
    q_gain,
    k_gain,
):
    model = tokens.shape[2]
    rows_here = q_weight.shape[0]
    members = 2 * lax.axis_size("s")
    q_cols, kv_cols = q_weight.shape[1], key_matrix.shape[1]
    heads = kv_cols // 64 // members
    chunks = len(CHUNKS)
    core = lax.axis_index("c")
    first_member = 2 * lax.axis_index("s")
    members_at = jnp.stack([first_member + core, first_member + 1 - core]).astype(jnp.int32)
    flip = jnp.stack([flip_at(), chip_at()]).astype(jnp.int32)

    attn_mine, attn_away = pack_call(
        functools.partial(pack_attn_kernel, heads),
        members_at,
        (heads + heads // 2, rows_here, 256),
        (q_weight, key_matrix, value_matrix, out_weight),
    )
    attn_own = core_pair(attn_mine, swap_core(attn_away), 256, 0, 1)
    attn_gather = Gather(attn_own)
    attn_blocks = attn_gather.blocks()
    ffn_cols = gate_weight.shape[1] // members
    tile = ffn_cols // sum(CHUNKS)
    ffn_mine, ffn_away = pack_call(
        pack_ffn_kernel, members_at, (3, rows_here, ffn_cols), (gate_weight, up_weight, down_weight)
    )
    ffn_other = swap_core(ffn_away)
    gathers = []
    for k, count in enumerate(CHUNKS):
        own_part = core_pair(ffn_mine, ffn_other, tile, sum(CHUNKS[:k]), count)
        if k == 0:
            before = attn_gather.first
        else:
            before = gathers[0].first if k == 1 else gathers[-1].second
        gathers.append(Gather(own_part, *before))

    high, low = positions // 128, positions % 128
    place_cols = jnp.stack([high, low], axis=2).astype(bf16)
    place_cols = jnp.pad(place_cols, ((0, 0), (0, 0), (0, 126)))
    tok = to_sequence(tokens, place_cols)
    quarters, size, _ = tok.shape
    own = quarters * size
    length = own * members
    tok = tok.reshape(own, model + 128)
    place_cols = tok[:, model:]
    tok = tok[:, :model].astype(f32)
    attn_gain_r = relative(attn_gain)
    ffn_gain_r = relative(ffn_gain)
    in_scale = rms_scale(tok)
    in_hat = tok * in_scale
    x = group_gather(jnp.concatenate([(in_hat * attn_gain_r).astype(bf16), place_cols], axis=1))
    x_t = [turn(a, model) for a in x]

    pos = [a[:, model : model + 2].astype(f32) for a in x]
    pos = jnp.stack([(p[:, 0] * 128.0 + p[:, 1]).reshape(quarters, size) for p in pos], axis=1)
    if pair_group():
        pos = jnp.where(core == 0, pos, pos[:, ::-1])
    inverse = rope_base ** (-(2.0 * jnp.arange(32, dtype=f32)) / 64)
    turned = pos.reshape(length)[:, None] * inverse[None, :]
    cosines = jnp.tile(jnp.cos(turned), (1, 4))
    sines = jnp.tile(jnp.sin(turned), (1, 4))
    q_gain2 = jnp.tile(q_gain, 2)[None]
    k_gain2 = jnp.tile(k_gain, 2)[None]

    cot_own = to_sequence(after(cotangent, x[0])).reshape(own, model)
    cot = group_gather(cot_own)
    cot_t = [turn(a, model) for a in cot]

    mixed = attention_call(
        flip, size, heads, x, cosines, sines, q_gain2, k_gain2, attn_blocks
    )
    out_w = jnp.concatenate(
        [
            jnp.concatenate([b[i, heads + j] for j in range(heads // 2)], axis=1)
            for b in attn_blocks
            for i in range(b.shape[0])
        ],
        axis=0,
    )
    mixed = [after(mixed[0], *gathers[0].first), *mixed[1:]]
    residual = tok + group_scatter([[dot(m, out_w, NT) for m in mixed]])
    residual = after(residual, *gathers[0].second)
    mid_scale = rms_scale(residual)
    mid_hat = residual * mid_scale
    mid = group_gather((mid_hat * ffn_gain_r).astype(bf16))
    mid_t = [turn(a, model) for a in mid]

    out_parts, mid_parts, sums = [], [], []

    def step_all(*which):
        return [a for i in which for a in sums[i].advance()]

    for k in range(chunks):
        waits = []
        if k == 0:
            waits = gathers[1].second
        elif k == 1:
            waits = gathers[2].first
        else:
            waits = step_all(0)
        if k:
            waits = waits + [mid_parts[-1][0]]
        parts = ffn_call(
            tile,
            CHUNKS[k],
            [after(mid[0], *waits), *mid[1:]],
            mid_t,
            cot,
            cot_t,
            gathers[k].blocks(),
        )
        out_parts.append(parts[:members])
        mid_parts.append(parts[members : 2 * members])
        sums.append(Reduction(parts[2 * members :]))

    d_mid = group_scatter(mid_parts)
    ffn_gain_part = jnp.sum(d_mid * mid_hat, axis=0)
    d_resid = cot_own.astype(f32) + norm_back(d_mid, mid_hat, mid_scale, ffn_gain_r)
    d_attn = group_gather(d_resid.astype(bf16))
    waits = step_all(0, 1) + step_all(0, 1)
    d_mixed = [dot(d, out_w).astype(bf16) for d in d_attn]
    d_attn_t = [turn(d, model) for d in d_attn]

    calls = 2 if heads % 4 == 0 else 1
    d_in_parts, gain_parts = [], []
    for call in range(calls):
        waits = waits + step_all(2) if call == 0 else step_all(0, 1, 2) + step_all(2)
        parts = attention_back_call(
            after(flip, *waits),
            size,
            call * (heads // calls),
            heads // calls,
            x,
            x_t,
            d_attn_t,
            mixed,
            cosines,
            sines,
            q_gain2,
            k_gain2,
            d_mixed,
            attn_blocks,
        )
        d_in_parts.append(parts[:members])
        gain_parts.append(parts[members])
        sums.append(Reduction(parts[members + 1 :]))
    head_gains = sum(gain_parts)
    waits = step_all(1, 2)
    out_parts[0] = [after(out_parts[0][0], d_in_parts[0][0]), *out_parts[0][1:]]
    d_in = group_scatter(d_in_parts)
    attn_gain_part = jnp.sum(d_in * in_hat, axis=0)
    input_grad = d_resid + norm_back(d_in, in_hat, in_scale, attn_gain_r)
    input_grad = input_grad.astype(bf16).reshape(quarters, size, model)
    if square():
        sums[-1].state[2] = after(sums[-1].state[2], input_grad, *waits)
    input_grad = from_sequence(input_grad)
    while any(r.step < 5 for r in sums):
        step_all(*[i for i, r in enumerate(sums) if r.step < 5])
    ffn_sums = [r.state for r in sums[:chunks]]
    heads_sums = [r.state for r in sums[chunks:]]

    output = (residual + group_scatter(out_parts)).astype(bf16)
    output = from_sequence(output.reshape(quarters, size, model))

    gain_sums = sum_all(
        jnp.concatenate(
            [
                relative(attn_gain_part),
                relative(ffn_gain_part),
                head_gains[0, :64] + head_gains[0, 64:],
                head_gains[1, :64],
            ]
        ),
        ffn_sums[-1][0],
    )

    if members == 2:
        ffn_grads = finish_ffn_call(ffn_sums)
        mine, other = heads_sums[-1]
        heads_sums[-1] = (after(mine, ffn_grads[0]), other)
        q_grad, k_grad, v_grad, out_grad = finish_heads_call(heads_sums)
    else:
        heads_all = [every_member(h) for h in heads_sums]
        every = jnp.concatenate([h[i] for i in range(members) for h in heads_all], axis=0)
        every = every.transpose(1, 0, 2).astype(f32)
        ffn_sums = [every_member(s) for s in ffn_sums]
        q_grad = every[:, :, :128].reshape(rows_here, q_cols)
        k_grad = every[:, :, 128:192].reshape(rows_here, kv_cols)
        v_grad = every[:, :, 192:256].reshape(rows_here, kv_cols)
        out_grad = every[:, :, 256:].reshape(rows_here, q_cols)
        ffn_grads = [
            jnp.concatenate(
                [ffn_sums[k][i][w] for i in range(members) for k in range(chunks)], axis=1
            ).astype(f32)
            for w in range(3)
        ]
    return (
        output,
        input_grad,
        q_grad,
        k_grad,
        v_grad,
        out_grad,
        ffn_grads[0],
        ffn_grads[1],
        ffn_grads[2],
        gain_sums[:model],
        gain_sums[model : 2 * model],
        gain_sums[2 * model : 2 * model + 64],
        gain_sums[2 * model + 64 :],
    )


def solution(mesh):
    dp, seq = mesh.devices.shape
    lines = 4
    fine = Mesh(mesh.devices.reshape(dp // 4, 2, 2, lines, seq // lines), EVERY)
    rows, cols = ("o", "x", "c"), ("z", "s")
    tokens = P(rows, cols, None)
    weight = P(rows, None)
    return jax.shard_map(
        local,
        mesh=fine,
        in_specs=(tokens, P(rows, cols), tokens) + (weight,) * 7 + (P(),) * 4,
        out_specs=(tokens, tokens) + (weight,) * 7 + (P(),) * 4,
        check_vma=False,
    )
```

```python
import functools

import jax
import jax.numpy as jnp
from jax import lax
from jax.experimental import pallas as pl
from jax.experimental.pallas import tpu as pltpu
from jax.sharding import Mesh, PartitionSpec as P

epsilon = 1e-05
rope_base = 1000000.0
f32 = jnp.float32
bf16 = jnp.bfloat16
SWAP = ((0, 1), (1, 0))
EVERY = ("o", "x", "c", "z", "s")
NT = (((1,), (1,)), ((), ()))
NN = (((1,), (0,)), ((), ()))


def dot(left, right, dims=NN):
    return lax.dot_general(left, right, dims, preferred_element_type=f32)


def rms_scale(rows):
    return lax.rsqrt(jnp.mean(rows * rows, axis=-1, keepdims=True) + epsilon)


def norm_back(grad_out, normed_hat, inv_scale, gain):
    scaled = grad_out * gain
    return inv_scale * (scaled - normed_hat * jnp.mean(scaled * normed_hat, axis=-1, keepdims=True))


def square():
    return lax.axis_size("o") == 2 and lax.axis_size("x") == 2


def pair_group():
    return lax.axis_size("s") == 1


def chip_at():
    if not square():
        return jnp.int32(0)
    return 2 * lax.axis_index("o") + lax.axis_index("x")


def flip_at():
    return lax.axis_index("c") if pair_group() else jnp.int32(0)


def relative(vector):
    if not square():
        return vector
    quarter = vector.shape[0] // 4
    blocks = [
        lax.dynamic_slice_in_dim(vector, (chip_at() ^ i) * quarter, quarter) for i in range(4)
    ]
    return jnp.concatenate(blocks)


def after(array, *others):
    return lax.optimization_barrier((array, *others))[0]


def swap_core(array):
    return lax.ppermute(array, "c", SWAP)


def group_gather(rows):
    if pair_group():
        return [rows, swap_core(rows)]
    full = lax.all_gather(rows, ("s", "c"), axis=0)
    return [full[i] for i in range(full.shape[0])]


def group_scatter(parts):
    if pair_group():
        away = sum(p[1].astype(f32) for p in parts).astype(bf16)
        return sum(p[0].astype(f32) for p in parts) + swap_core(away).astype(f32)
    total = jnp.stack([sum(p[m].astype(f32) for p in parts) for m in range(len(parts[0]))])
    return lax.psum_scatter(total, ("s", "c"), scatter_dimension=0, tiled=False)


def merge_kernel(relate, at_ref, mine_ref, other_ref, out_ref):
    core, chip = at_ref[0], at_ref[1]
    if not relate:
        out_ref[:, core] = mine_ref[...]
        out_ref[:, 1 - core] = other_ref[...]
        return
    quarter = mine_ref.shape[-1] // 4
    for r in range(4):
        to = pl.ds(pl.multiple_of((chip ^ r) * quarter, quarter), quarter)
        at = slice(r * quarter, (r + 1) * quarter)
        out_ref[:, core, :, to] = mine_ref[:, :, at]
        out_ref[:, 1 - core, :, to] = other_ref[:, :, at]


def smem():
    return pl.BlockSpec(memory_space=pltpu.SMEM)


def place():
    return jnp.stack([lax.axis_index("c"), chip_at()]).astype(jnp.int32)


def small_cost(bytes_moved):
    return pl.CostEstimate(flops=0, bytes_accessed=bytes_moved, transcendentals=0)


def by_core(mine, other, relate=False):
    n, rows, width = mine.shape
    step = 1 if n % 3 else n // 3
    block = pl.BlockSpec((step, rows, width), lambda i: (i, 0, 0))
    out = pl.pallas_call(
        functools.partial(merge_kernel, relate),
        grid=(n // step,),
        in_specs=[smem(), block, block],
        out_specs=pl.BlockSpec((step, 2, rows, width), lambda i: (i, 0, 0, 0)),
        out_shape=jax.ShapeDtypeStruct((n, 2, rows, width), mine.dtype),
        cost_estimate=small_cost(mine.size * 8),
        compiler_params=pltpu.CompilerParams(vmem_limit_bytes=32 * 2**20),
        name="merge",
    )(place(), mine, other)
    return out.reshape(n, 2 * rows, width)


def enter_kernel(at_ref, rows_ref, *refs):
    core, chip = at_ref[0], at_ref[1]
    mine_ref, away_ref = refs[-2:]
    size = mine_ref.shape[1]
    model = rows_ref.shape[-1]
    quarter = model // 4
    for ref, which in ((mine_ref, core), (away_ref, 1 - core)):
        span = pl.ds(pl.multiple_of(which * size, size), size)
        for r in range(4):
            at = pl.ds(pl.multiple_of((chip ^ r) * quarter, quarter), quarter)
            ref[:, :, r * quarter : (r + 1) * quarter] = rows_ref[:, span, at]
        if len(refs) == 3:
            ref[:, :, model:] = refs[0][:, span, :]


def to_sequence(rows, *extra):
    seqs, count, width = rows.shape
    width += sum(e.shape[2] for e in extra)
    half = jax.ShapeDtypeStruct((seqs, count // 2, width), rows.dtype)
    mine, away = pl.pallas_call(
        enter_kernel,
        in_specs=[smem()] + [pl.BlockSpec(memory_space=pltpu.VMEM)] * (1 + len(extra)),
        out_specs=[pl.BlockSpec(memory_space=pltpu.VMEM)] * 2,
        out_shape=[half, half],
        cost_estimate=small_cost(rows.size * 4),
        name="enter",
    )(place(), rows, *extra)
    other = swap_core(away)
    every = by_core(mine.reshape(1, -1, width), other.reshape(1, -1, width))
    return lax.all_to_all(every.reshape(2 * seqs, count // 2, width), "z", 0, 0, tiled=True)


def from_sequence(rows):
    core = lax.axis_index("c")
    every = lax.all_to_all(rows, "z", 0, 0, tiled=True)
    seqs = every.shape[0] // 2
    away = lax.dynamic_slice_in_dim(every, (1 - core) * seqs, seqs)
    mine = lax.dynamic_slice_in_dim(every, core * seqs, seqs)
    return by_core(mine, swap_core(away), relate=True)


def pair_kernel(at_ref, mine_ref, other_ref, out_ref):
    core = at_ref[0]
    out_ref[core] = mine_ref[...]
    out_ref[1 - core] = other_ref[...]


def core_pair(mine, other, tile, start, count):
    n, rows, _ = mine.shape
    block = pl.BlockSpec((n, rows, tile), lambda i: (0, 0, start + i))
    return pl.pallas_call(
        pair_kernel,
        grid=(count,),
        in_specs=[smem(), block, block],
        out_specs=pl.BlockSpec((2, n, rows, tile), lambda i: (0, 0, 0, i)),
        out_shape=jax.ShapeDtypeStruct((2, n, rows, count * tile), mine.dtype),
        cost_estimate=small_cost(8 * n * rows * count * tile),
        name="core_pair",
    )(place(), mine, other)


class Gather:
    def __init__(self, own, *before):
        self.own = own
        if square():
            own = after(own, *before)
            self.first = [lax.ppermute(own, "x", SWAP), lax.ppermute(own, "o", SWAP)]
            by_x, by_o = self.first
            self.second = [
                lax.ppermute(by_x[:1], "o", SWAP),
                lax.ppermute(by_o[1:], "x", SWAP),
            ]
        else:
            self.first = self.second = []

    def blocks(self):
        if square():
            return [self.own, *self.first, *self.second]
        full = lax.all_gather(self.own, ("o", "x"), axis=0, tiled=True)
        return [full[i : i + 2] for i in range(0, full.shape[0], 2)]


def grad_slots(model):
    if square():
        return [(2, 0), (3, 0), (0, 0), (3, 1), (2, 1), (1, 0), (0, 1), (1, 1)], [2, 2, 2, 2]
    return [(0, i) for i in range(8)], [8]


def put_rows(out_refs, slots, index, cols, term):
    size = term.shape[0] // 8
    for part, (which, row) in enumerate(slots):
        out_refs[which][index, row * size : (row + 1) * size, cols] = term[
            part * size : (part + 1) * size
        ].astype(bf16)


def add_up(*terms):
    return functools.reduce(jnp.add, [t.astype(f32) for t in terms]).astype(bf16)


def combine_kernel(keep_a, come_a, last_a, keep_b, come_b, last_b, out_ref):
    half = last_a.shape[1]
    for at, (keep, come, last) in enumerate(((keep_a, come_a, last_a), (keep_b, come_b, last_b))):
        out_ref[:, at * half : (at + 1) * half, :] = add_up(keep[...], come[...], last[...])


def combine(keep_a, come_a, last_a, keep_b, come_b, last_b):
    n, half, width = last_a.shape
    block = pl.BlockSpec((1, half, width), lambda i: (i, 0, 0))
    return pl.pallas_call(
        combine_kernel,
        grid=(n,),
        in_specs=[block] * 6,
        out_specs=pl.BlockSpec((1, 2 * half, width), lambda i: (i, 0, 0)),
        out_shape=jax.ShapeDtypeStruct((n, 2 * half, width), bf16),
        cost_estimate=small_cost(16 * n * half * width),
        name="combine",
    )(keep_a, come_a, last_a, keep_b, come_b, last_b)


class Reduction:
    def __init__(self, outs):
        self.step = 0
        self.state = outs
        if square():
            self.state = [
                *outs,
                lax.ppermute(outs[0], "x", SWAP),
                lax.ppermute(outs[1], "o", SWAP),
            ]

    def advance(self):
        step, self.step = self.step, self.step + 1
        state = self.state
        on_line = lax.axis_size("z") == 4
        if step == 0 and square():
            _, _, keep_a, keep_b, come_a, come_b = state
            half = keep_a.shape[1] // 2
            go_a = add_up(keep_a[:, half:], come_a[:, half:])
            go_b = add_up(keep_b[:, half:], come_b[:, half:])
            last_a, last_b = lax.ppermute(go_a, "o", SWAP), lax.ppermute(go_b, "x", SWAP)
            self.state = (keep_a, come_a, last_a, keep_b, come_b, last_b)
            return [go_a, go_b]
        if step == 1:
            if square():
                here = combine(*state)
            else:
                here = lax.psum_scatter(
                    state[0].astype(f32), ("o", "x"), scatter_dimension=1, tiled=True
                ).astype(bf16)
            come = lax.ppermute(here, "z", ((0, 1), (3, 2))) if on_line else None
            self.state = (here, come)
            return [here]
        if step == 2 and on_line:
            here = add_up(*state)
            self.state = (here, lax.ppermute(here, "z", ((1, 2), (2, 1))))
            return [here]
        if step == 3 and on_line:
            here = add_up(*state)
            self.state = (here, lax.ppermute(here, "z", ((1, 0), (2, 3))))
            return [here]
        if step == 4:
            if on_line:
                at = lax.axis_index("z")
                total = jnp.where((at == 0) | (at == 3), state[1], state[0])
            else:
                total = lax.psum(state[0].astype(f32), "z").astype(bf16)
            core = lax.axis_index("c")
            half = total.shape[1] // 2
            mine = lax.dynamic_slice_in_dim(total, core * half, half, 1)
            away = lax.dynamic_slice_in_dim(total, (1 - core) * half, half, 1)
            self.state = (mine, swap_core(away))
            return [total]
        return []


def every_member(done):
    mine, other = done
    first = lax.axis_index("c") == 0
    pair = jnp.stack([jnp.where(first, mine, other), jnp.where(first, other, mine)])
    every = lax.all_gather(pair, "s", axis=0, tiled=True)
    return [every[i] for i in range(every.shape[0])]


def sum_all(terms, before):
    if not (square() and pair_group() and lax.axis_size("z") == 4):
        return lax.psum(terms, EVERY)
    for axis, perm in (
        ("c", SWAP),
        ("x", SWAP),
        ("o", SWAP),
        ("z", ((0, 1), (1, 0), (2, 3), (3, 2))),
        ("z", ((0, 2), (2, 0), (1, 3), (3, 1))),
    ):
        if axis == "z":
            terms = after(terms, before)
        terms = terms + lax.ppermute(terms, axis, perm)
    return terms


def member_cols(start, count):
    return pl.ds(pl.multiple_of(start, 128), count)


def pack_attn_kernel(heads, at_ref, q_ref, k_ref, v_ref, o_ref, *outs):
    for i in range(2):
        member, attn_ref = at_ref[i], outs[i]
        for j in range(0, heads, 2):
            head = member * heads + j
            keys = k_ref[:, member_cols(head * 64, 128)]
            values = v_ref[:, member_cols(head * 64, 128)]
            for m in range(2):
                attn_ref[j + m, :, :128] = q_ref[:, member_cols((head + m) * 128, 128)]
                attn_ref[j + m, :, 128:192] = keys[:, m * 64 : (m + 1) * 64]
                attn_ref[j + m, :, 192:] = values[:, m * 64 : (m + 1) * 64]
        for j in range(heads // 2):
            attn_ref[heads + j] = o_ref[:, member_cols(member * heads * 128 + j * 256, 256)]


def pack_ffn_kernel(at_ref, g_ref, u_ref, d_ref, *outs):
    for i in range(2):
        width = outs[i].shape[2]
        for w, ref in enumerate((g_ref, u_ref, d_ref)):
            outs[i][w] = ref[:, member_cols(at_ref[i] * width, width)]


def pack_call(kernel, members_at, out, weights):
    return pl.pallas_call(
        kernel,
        in_specs=[smem()] + [pl.BlockSpec(memory_space=pltpu.VMEM)] * len(weights),
        out_specs=[pl.BlockSpec(memory_space=pltpu.VMEM)] * 2,
        out_shape=[jax.ShapeDtypeStruct(out, bf16)] * 2,
        cost_estimate=small_cost(2 * 4 * out[0] * out[1] * out[2]),
        compiler_params=pltpu.CompilerParams(vmem_limit_bytes=32 * 2**20),
        name="pack",
    )(members_at, *weights)


def finish_ffn_kernel(at_ref, *refs):
    mines, others, outs = refs[:-3:2], refs[1:-3:2], refs[-3:]
    first = at_ref[0] == 0
    total = sum(m.shape[2] for m in mines)
    start = 0
    for mine_ref, other_ref in zip(mines, others):
        width = mine_ref.shape[2]
        mine, other = mine_ref[0], other_ref[0]
        low = jnp.where(first, mine, other).astype(f32)
        high = jnp.where(first, other, mine).astype(f32)
        for w in range(3):

            @pl.when(pl.program_id(0) == w)
            def _():
                outs[w][:, start : start + width] = low
                outs[w][:, total + start : total + start + width] = high

        start += width


def finish_ffn_call(sums):
    rows = sums[0][0].shape[1]
    out = jax.ShapeDtypeStruct((rows, 2 * sum(s[0].shape[2] for s in sums)), f32)
    arrays = [a for s in sums for a in s]
    return pl.pallas_call(
        finish_ffn_kernel,
        grid=(3,),
        in_specs=[smem()] + [pl.BlockSpec((1, *a.shape[1:]), lambda w: (w, 0, 0)) for a in arrays],
        out_specs=[whole_spec(out.shape)] * 3,
        out_shape=[out] * 3,
        cost_estimate=small_cost(out.size * 18),
        compiler_params=pltpu.CompilerParams(vmem_limit_bytes=40 * 2**20),
        name="finish_ffn",
    )(place(), *arrays)


def finish_heads_kernel(calls, at_ref, *refs):
    first = at_ref[0] == 0
    q_ref, k_ref, v_ref, o_ref = refs[2 * calls :]
    per_call = refs[0].shape[0]
    heads = calls * per_call

    def pick(head):
        mine, other = refs[2 * (head // per_call)], refs[2 * (head // per_call) + 1]
        mine, other = mine[head % per_call], other[head % per_call]
        return [
            jnp.where(first, mine, other).astype(f32),
            jnp.where(first, other, mine).astype(f32),
        ]

    for j in range(0, heads, 2):
        pairs = [pick(j), pick(j + 1)]
        for g in range(2):
            pair = [p[g] for p in pairs]
            head = g * heads + j
            for m in range(2):
                at = slice((head + m) * 128, (head + m + 1) * 128)
                q_ref[:, at] = pair[m][:, :128]
                o_ref[:, at] = pair[m][:, 256:]
            at = slice(head * 64, (head + 2) * 64)
            k_ref[:, at] = jnp.concatenate([p[:, 128:192] for p in pair], axis=1)
            v_ref[:, at] = jnp.concatenate([p[:, 192:256] for p in pair], axis=1)


def finish_heads_call(heads_sums):
    per_call, rows, _ = heads_sums[0][0].shape
    heads = per_call * len(heads_sums)
    wide = jax.ShapeDtypeStruct((rows, heads * 256), f32)
    narrow = jax.ShapeDtypeStruct((rows, heads * 128), f32)
    return pl.pallas_call(
        functools.partial(finish_heads_kernel, len(heads_sums)),
        in_specs=[smem()] + [pl.BlockSpec(memory_space=pltpu.VMEM)] * (2 * len(heads_sums)),
        out_specs=[pl.BlockSpec(memory_space=pltpu.VMEM)] * 4,
        out_shape=[wide, narrow, narrow, wide],
        cost_estimate=small_cost(rows * heads * 768 * 6),
        name="finish_heads",
    )(place(), *[a for s in heads_sums for a in s])


def fill(scratch, refs, index):
    row = 0
    for ref in refs:
        for part in range(ref.shape[0]):
            block = ref[part, index]
            scratch[row : row + block.shape[0], :] = block
            row += block.shape[0]


def ffn_kernel(members, blocks, slots, steps, *refs):
    xs, xts, cots, cotts = [refs[i * members : (i + 1) * members] for i in range(4)]
    rest = refs[4 * members :]
    weights, rest = rest[:blocks], rest[blocks:]
    out_refs, mid_refs = rest[:members], rest[members : 2 * members]
    grads = rest[2 * members : -8]
    gate, up, down, hid, dgate, dup, out_acc, mid_acc = rest[-8:]
    step = pl.program_id(0)
    for i, scratch in enumerate((gate, up, down)):
        fill(scratch, weights, i)

    @pl.when(step == 0)
    def _():
        out_acc[...] = jnp.zeros_like(out_acc)
        mid_acc[...] = jnp.zeros_like(mid_acc)

    own = xs[0].shape[0]
    rows = 512
    for m in range(members):

        def body(i, carry):
            at = pl.ds(pl.multiple_of(i * rows, rows), rows)
            to = pl.ds(pl.multiple_of(m * own + i * rows, rows), rows)
            x = xs[m][at, :]
            g = dot(x, gate[...])
            u = dot(x, up[...])
            dh = dot(cots[m][at, :], down[...])
            sig = jax.nn.sigmoid(g)
            act = g * sig
            h = (act * u).astype(bf16)
            dg = (dh * u * sig * (1.0 + g * (1.0 - sig))).astype(bf16)
            du = (dh * act).astype(bf16)
            hid[to, :] = h
            dgate[to, :] = dg
            dup[to, :] = du
            out_acc[to, :] += dot(h, down[...], NT)
            mid_acc[to, :] += dot(dg, gate[...], NT) + dot(du, up[...], NT)
            return carry

        lax.fori_loop(0, own // rows, body, 0)

    def over_rows(lefts, at, right):
        return functools.reduce(
            jnp.add,
            [dot(l[at, :], right[m * own : (m + 1) * own, :]) for m, l in enumerate(lefts)],
        )

    model = xts[0].shape[0]
    for i, (lefts, right) in enumerate(((xts, dgate), (xts, dup), (cotts, hid))):
        term = over_rows(lefts, slice(0, model), right)
        put_rows(grads, slots, i, slice(None), term)

    @pl.when(step == steps - 1)
    def _():
        for m in range(members):
            out_refs[m][...] = out_acc[m * own : (m + 1) * own, :].astype(bf16)
            mid_refs[m][...] = mid_acc[m * own : (m + 1) * own, :].astype(bf16)


def turn_kernel(in_ref, out_ref):
    out_ref[...] = in_ref[...].T


def turn(rows, width):
    count = rows.shape[0]
    return pl.pallas_call(
        turn_kernel,
        grid=(2,),
        in_specs=[pl.BlockSpec((count, width // 2), lambda i: (0, i))],
        out_specs=pl.BlockSpec((width // 2, count), lambda i: (i, 0)),
        out_shape=jax.ShapeDtypeStruct((width, count), rows.dtype),
        cost_estimate=small_cost(rows.size * 4),
        name="turn",
    )(rows)


def whole_spec(shape):
    zeros = (0,) * len(shape)
    return pl.BlockSpec(shape, lambda *_: zeros)


def single_spec(shape):
    zeros = (0,) * len(shape)
    return pl.BlockSpec(shape, lambda *_: zeros, pipeline_mode=pl.Buffered(1))


SHARE = 32

CHUNKS = (3, 3, 3)


def ffn_call(tile, steps, x, x_t, cot, cot_t, weights):
    members = len(x)
    own, model = x[0].shape
    rows = own * members
    width = steps * tile
    slots, heights = grad_slots(model)
    size = model // 8
    return pl.pallas_call(
        functools.partial(ffn_kernel, members, len(weights), slots, steps),
        grid=(steps,),
        in_specs=[single_spec((own, model))] * members
        + [single_spec(a.shape) for a in (*x_t, *cot, *cot_t)]
        + [
            pl.BlockSpec((w.shape[0], 3, w.shape[2], tile), lambda j: (0, 0, 0, j))
            for w in weights
        ],
        out_specs=[single_spec((own, model))] * (2 * members)
        + [pl.BlockSpec((3, n * size, tile), lambda j: (0, 0, j)) for n in heights],
        out_shape=[jax.ShapeDtypeStruct((own, model), bf16)] * (2 * members)
        + [jax.ShapeDtypeStruct((3, n * size, width), bf16) for n in heights],
        scratch_shapes=[pltpu.VMEM((model, tile), bf16)] * 3
        + [pltpu.VMEM((rows, tile), bf16)] * 3
        + [pltpu.VMEM((rows, model), f32)] * 2,
        compiler_params=pltpu.CompilerParams(vmem_limit_bytes=58 * 2**20),
        cost_estimate=pl.CostEstimate(
            flops=18 * rows * model * width // SHARE,
            bytes_accessed=(6 * rows * model * 2 + 12 * model * width) // SHARE,
            transcendentals=rows * width // SHARE,
        ),
        name="ffn",
    )(*x, *x_t, *cot, *cot_t, *weights)


def lanes_first():
    return lax.broadcasted_iota(jnp.int32, (1, 128), 1) < 64


def head_mean(square_terms):
    first = lanes_first()
    low = jnp.sum(jnp.where(first, square_terms, 0.0), axis=-1, keepdims=True)
    high = jnp.sum(jnp.where(first, 0.0, square_terms), axis=-1, keepdims=True)
    return jnp.where(first, low, high) * (1.0 / 64)


def partner(u):
    low = (lax.broadcasted_iota(jnp.int32, (1, 128), 1) & 63) < 32
    return jnp.where(low, -pltpu.roll(u, 96, 1), pltpu.roll(u, 32, 1))


def natural_rows(flip, members, own, size):
    for m in range(members):
        for i in range(own // size):
            to = pl.multiple_of((i * members + (m ^ flip)) * size, size)
            yield m, i * size, pl.ds(to, size)


def project(flip, size, xs, weights, w_scr, qkv):
    fill(w_scr, weights, 0)
    own = xs[0].shape[0]
    terms = [dot(x[...], w_scr[...]) for x in xs]
    for m, row, at in natural_rows(flip, len(xs), own, size):
        qkv[at, :] = terms[m][row : row + size]


def heads_of(u, gain, cosines, sines):
    inv = lax.rsqrt(head_mean(u * u) + epsilon)
    hat = u * inv
    turned = hat * gain
    return inv, hat, turned * cosines + partner(turned) * sines


def stack_heads(block):
    return jnp.concatenate([block[:, :64], block[:, 64:]], axis=0)


def unstack_heads(turned):
    half = turned.shape[1] // 2
    return jnp.concatenate([turned[:, :half], turned[:, half:]], axis=0).T


BLOCK = 256


def probs_of(q2, keys, block):
    parts = []
    for at in range(block + 1):
        parts.append(dot(keys[at * BLOCK : (at + 1) * BLOCK, :], q2, NT))
    key_at = lax.broadcasted_iota(jnp.int32, parts[-1].shape, 0)
    query_at = lax.broadcasted_iota(jnp.int32, parts[-1].shape, 1) & (BLOCK - 1)
    parts[-1] = jnp.where(key_at <= query_at, parts[-1], -1e30)
    top = functools.reduce(jnp.maximum, [jnp.max(p, axis=0, keepdims=True) for p in parts])
    parts = [jnp.exp(p - top) for p in parts]
    total = functools.reduce(jnp.add, [jnp.sum(p, axis=0, keepdims=True) for p in parts])
    inv = 1.0 / total
    return [p * inv for p in parts]


def attention_kernel(members, blocks, size, at_ref, *refs):
    xs, rest = refs[:members], refs[members:]
    cos_ref, sin_ref, qg_ref, kg_ref = rest[:4]
    weights, rest = rest[4 : 4 + blocks], rest[4 + blocks :]
    mixed_refs, rest = rest[:members], rest[members:]
    w_scr, qkv, q_scr, k_scr, vt_scr, mixed_scr = rest
    flip = at_ref[0]
    project(flip, size, xs, weights, w_scr, qkv)
    cosines, sines = cos_ref[...], sin_ref[...]
    _, _, q = heads_of(qkv[:, :128], qg_ref[...], cosines, sines)
    q_scr[...] = q.astype(bf16) * jnp.asarray(0.125, bf16)
    _, _, k = heads_of(qkv[:, 128:], kg_ref[...], cosines, sines)
    k_scr[...] = k[:, :64].astype(bf16)
    vt_scr[...] = qkv[:, 192:].astype(bf16).T
    for block in range(q_scr.shape[0] // BLOCK):
        at = slice(block * BLOCK, (block + 1) * BLOCK)
        q2 = stack_heads(q_scr[at, :])
        probs = probs_of(q2, k_scr, block)
        total = None
        for i, p in enumerate(probs):
            term = dot(vt_scr[:, i * BLOCK : (i + 1) * BLOCK], p.astype(bf16))
            total = term if total is None else total + term
        mixed_scr[at, :] = unstack_heads(total).astype(bf16)
    for m, row, at in natural_rows(flip, members, xs[0].shape[0], size):
        mixed_refs[m][row : row + size, :] = mixed_scr[at, :]


def attention_back_kernel(members, blocks, slots, steps, size, at_ref, *refs):
    xs, xts, das, mixes = [refs[i * members : (i + 1) * members] for i in range(4)]
    rest = refs[4 * members :]
    cos_ref, sin_ref, qg_ref, kg_ref = rest[:4]
    dms, rest = rest[4 : 4 + members], rest[4 + members :]
    weights, rest = rest[:blocks], rest[blocks:]
    din_refs, gains_ref, grads = rest[:members], rest[members], rest[members + 1 : -12]
    rest = rest[-12:]
    w_scr, qkv, q_scr, k_scr, v_scr, kt_scr, dm_scr, dq_scr, dkv_scr, dall, dqkv, din_acc = rest
    flip = at_ref[0]
    own = xs[0].shape[0]
    step = pl.program_id(0)
    project(flip, size, xs, weights, w_scr, qkv)
    for m, row, at in natural_rows(flip, members, own, size):
        dm_scr[at, :] = dms[m][row : row + size, :]
    cosines, sines = cos_ref[...], sin_ref[...]
    q_gain, k_gain = qg_ref[...], kg_ref[...]
    q_inv, q_hat, q = heads_of(qkv[:, :128], q_gain, cosines, sines)
    q_scr[...] = q.astype(bf16) * jnp.asarray(0.125, bf16)
    k_inv, k_hat, k = heads_of(qkv[:, 128:], k_gain, cosines, sines)
    k_scr[...] = k[:, :64].astype(bf16)
    kt_scr[...] = k[:, :64].astype(bf16).T
    v_scr[...] = qkv[:, 192:].astype(bf16)
    dkv_scr[...] = jnp.zeros_like(dkv_scr)
    for block in range(q_scr.shape[0] // BLOCK):
        at = slice(block * BLOCK, (block + 1) * BLOCK)
        q2 = stack_heads(q_scr[at, :])
        do2 = stack_heads(dm_scr[at, :])
        probs = probs_of(q2, k_scr, block)
        backs = [
            dot(v_scr[i * BLOCK : (i + 1) * BLOCK, :], do2, NT) for i in range(block + 1)
        ]
        delta = functools.reduce(
            jnp.add, [jnp.sum(p * b, axis=0, keepdims=True) for p, b in zip(probs, backs)]
        )
        total = None
        for i, (p, b) in enumerate(zip(probs, backs)):
            ds = (p * (b - delta)).astype(bf16)
            keys = slice(i * BLOCK, (i + 1) * BLOCK)
            term = dot(kt_scr[:, keys], ds)
            total = term if total is None else total + term
            dkv_scr[keys, :] += jnp.concatenate([dot(ds, q2), dot(p.astype(bf16), do2)], axis=1)
        dq_scr[at, :] = unstack_heads(total) * 0.125
    first = lanes_first()
    dq = dq_scr[...].astype(bf16).astype(f32)
    dkv = dkv_scr[...].astype(bf16).astype(f32)
    dq = dq * cosines - partner(dq) * sines
    dk = dkv * cosines - partner(dkv) * sines
    q_part = jnp.sum(dq * q_hat, axis=0, keepdims=True)
    k_part = jnp.sum(jnp.where(first, dk * k_hat, 0.0), axis=0, keepdims=True)
    both = jnp.concatenate([q_part, k_part], axis=0)

    @pl.when(step == 0)
    def _():
        gains_ref[...] = both
        din_acc[...] = jnp.zeros_like(din_acc)

    @pl.when(step > 0)
    def _():
        gains_ref[...] += both

    scaled = dq * q_gain
    d_q = q_inv * (scaled - q_hat * head_mean(scaled * q_hat))
    scaled = dk * k_gain
    d_k = k_inv * (scaled - k_hat * head_mean(scaled * k_hat))
    dall[:, :128] = d_q.astype(bf16)
    dall[:, 128:] = jnp.where(first, d_k, dkv).astype(bf16)
    for m, row, at in natural_rows(flip, members, own, size):
        dqkv[m * own + row : m * own + row + size, :] = dall[at, :]
    din_acc[...] += dot(dqkv[...], w_scr[...], NT)
    term = sum(dot(xt[...], dqkv[m * own : (m + 1) * own, :]) for m, xt in enumerate(xts))
    put_rows(grads, slots, 0, slice(0, 256), term)
    term = sum(dot(da[...], mix[...]) for da, mix in zip(das, mixes))
    put_rows(grads, slots, 0, slice(256, 384), term)

    @pl.when(step == steps - 1)
    def _():
        for m in range(members):
            din_refs[m][...] = din_acc[m * own : (m + 1) * own, :].astype(bf16)


def attention_cost(length, heads, model, products):
    return pl.CostEstimate(
        flops=heads * (products * 2 * length * length * 64 + 2 * length * model * 256) // SHARE,
        bytes_accessed=4 * length * model * 2 // SHARE,
        transcendentals=heads * 2 * length * length // SHARE,
    )


def weight_specs(weights, start=0):
    return [
        pl.BlockSpec((w.shape[0], 1, w.shape[2], 256), lambda j: (0, j + start, 0, 0))
        for w in weights
    ]


def attention_call(flip, size, heads, x, cosines, sines, q_gain, k_gain, weights):
    members = len(x)
    own, model = x[0].shape[0], 128 * (x[0].shape[1] // 128 - 1)
    length = members * own
    return pl.pallas_call(
        functools.partial(attention_kernel, members, len(weights), size),
        grid=(heads,),
        in_specs=[smem()]
        + [single_spec((own, model))] * members
        + [single_spec(a.shape) for a in (cosines, sines, q_gain, k_gain)]
        + weight_specs(weights),
        out_specs=[pl.BlockSpec((own, 128), lambda j: (0, j))] * members,
        out_shape=[jax.ShapeDtypeStruct((own, heads * 128), bf16)] * members,
        scratch_shapes=[
            pltpu.VMEM((model, 256), bf16),
            pltpu.VMEM((length, 256), f32),
            pltpu.VMEM((length, 128), bf16),
            pltpu.VMEM((length, 64), bf16),
            pltpu.VMEM((64, length), bf16),
            pltpu.VMEM((length, 128), bf16),
        ],
        compiler_params=pltpu.CompilerParams(vmem_limit_bytes=48 * 2**20),
        cost_estimate=attention_cost(length, heads, model, 4),
        name="attention",
    )(flip, *x, cosines, sines, q_gain, k_gain, *weights)


def attention_back_call(
    flip, size, start, heads, x, x_t, d_attn_t, mixed, cosines, sines, q_gain, k_gain, d_mixed, weights
):
    members = len(x)
    own, model = x_t[0].shape[1], x_t[0].shape[0]
    length = members * own
    slots, heights = grad_slots(model)
    eighth = model // 8
    return pl.pallas_call(
        functools.partial(attention_back_kernel, members, len(weights), slots, heads, size),
        grid=(heads,),
        in_specs=[smem()]
        + [single_spec(s) for s in [(own, model)] * members + [(model, own)] * (2 * members)]
        + [pl.BlockSpec((own, 128), lambda j: (0, j + start))] * members
        + [single_spec(a.shape) for a in (cosines, sines, q_gain, k_gain)]
        + [pl.BlockSpec((own, 128), lambda j: (0, j + start))] * members
        + weight_specs(weights, start),
        out_specs=[single_spec((own, model))] * members
        + [whole_spec((2, 128))]
        + [pl.BlockSpec((1, n * eighth, 384), lambda j: (j, 0, 0)) for n in heights],
        out_shape=[jax.ShapeDtypeStruct((own, model), bf16)] * members
        + [jax.ShapeDtypeStruct((2, 128), f32)]
        + [jax.ShapeDtypeStruct((heads, n * eighth, 384), bf16) for n in heights],
        scratch_shapes=[
            pltpu.VMEM((model, 256), bf16),
            pltpu.VMEM((length, 256), f32),
            pltpu.VMEM((length, 128), bf16),
            pltpu.VMEM((length, 64), bf16),
            pltpu.VMEM((length, 64), bf16),
            pltpu.VMEM((64, length), bf16),
            pltpu.VMEM((length, 128), bf16),
            pltpu.VMEM((length, 128), f32),
            pltpu.VMEM((length, 128), f32),
            pltpu.VMEM((length, 256), bf16),
            pltpu.VMEM((length, 256), bf16),
            pltpu.VMEM((length, model), f32),
        ],
        compiler_params=pltpu.CompilerParams(vmem_limit_bytes=58 * 2**20),
        cost_estimate=attention_cost(length, heads, model, 10),
        name="attention_back",
    )(flip, *x, *x_t, *d_attn_t, *mixed, cosines, sines, q_gain, k_gain, *d_mixed, *weights)


def local(
    tokens,
    positions,
    cotangent,
    q_weight,
    key_matrix,
    value_matrix,
    out_weight,
    gate_weight,
    up_weight,
    down_weight,
    attn_gain,
    ffn_gain,
    q_gain,
    k_gain,
):
    model = tokens.shape[2]
    rows_here = q_weight.shape[0]
    members = 2 * lax.axis_size("s")
    q_cols, kv_cols = q_weight.shape[1], key_matrix.shape[1]
    heads = kv_cols // 64 // members
    chunks = len(CHUNKS)
    core = lax.axis_index("c")
    first_member = 2 * lax.axis_index("s")
    members_at = jnp.stack([first_member + core, first_member + 1 - core]).astype(jnp.int32)
    flip = jnp.stack([flip_at(), chip_at()]).astype(jnp.int32)

    attn_mine, attn_away = pack_call(
        functools.partial(pack_attn_kernel, heads),
        members_at,
        (heads + heads // 2, rows_here, 256),
        (q_weight, key_matrix, value_matrix, out_weight),
    )
    attn_own = core_pair(attn_mine, swap_core(attn_away), 256, 0, 1)
    attn_gather = Gather(attn_own)
    attn_blocks = attn_gather.blocks()
    ffn_cols = gate_weight.shape[1] // members
    tile = ffn_cols // sum(CHUNKS)
    ffn_mine, ffn_away = pack_call(
        pack_ffn_kernel, members_at, (3, rows_here, ffn_cols), (gate_weight, up_weight, down_weight)
    )
    ffn_other = swap_core(ffn_away)
    gathers = []
    for k, count in enumerate(CHUNKS):
        own_part = core_pair(ffn_mine, ffn_other, tile, sum(CHUNKS[:k]), count)
        if k == 0:
            before = attn_gather.first
        else:
            before = gathers[0].first if k == 1 else gathers[-1].second
        gathers.append(Gather(own_part, *before))

    high, low = positions // 128, positions % 128
    place_cols = jnp.stack([high, low], axis=2).astype(bf16)
    place_cols = jnp.pad(place_cols, ((0, 0), (0, 0), (0, 126)))
    tok = to_sequence(tokens, place_cols)
    quarters, size, _ = tok.shape
    own = quarters * size
    length = own * members
    tok = tok.reshape(own, model + 128)
    place_cols = tok[:, model:]
    tok = tok[:, :model].astype(f32)
    attn_gain_r = relative(attn_gain)
    ffn_gain_r = relative(ffn_gain)
    in_scale = rms_scale(tok)
    in_hat = tok * in_scale
    x = group_gather(jnp.concatenate([(in_hat * attn_gain_r).astype(bf16), place_cols], axis=1))
    x_t = [turn(a, model) for a in x]

    pos = [a[:, model : model + 2].astype(f32) for a in x]
    pos = jnp.stack([(p[:, 0] * 128.0 + p[:, 1]).reshape(quarters, size) for p in pos], axis=1)
    if pair_group():
        pos = jnp.where(core == 0, pos, pos[:, ::-1])
    inverse = rope_base ** (-(2.0 * jnp.arange(32, dtype=f32)) / 64)
    turned = pos.reshape(length)[:, None] * inverse[None, :]
    cosines = jnp.tile(jnp.cos(turned), (1, 4))
    sines = jnp.tile(jnp.sin(turned), (1, 4))
    q_gain2 = jnp.tile(q_gain, 2)[None]
    k_gain2 = jnp.tile(k_gain, 2)[None]

    cot_own = to_sequence(after(cotangent, x[0])).reshape(own, model)
    cot = group_gather(cot_own)
    cot_t = [turn(a, model) for a in cot]

    mixed = attention_call(
        flip, size, heads, x, cosines, sines, q_gain2, k_gain2, attn_blocks
    )
    out_w = jnp.concatenate(
        [
            jnp.concatenate([b[i, heads + j] for j in range(heads // 2)], axis=1)
            for b in attn_blocks
            for i in range(b.shape[0])
        ],
        axis=0,
    )
    mixed = [after(mixed[0], *gathers[0].first), *mixed[1:]]
    residual = tok + group_scatter([[dot(m, out_w, NT) for m in mixed]])
    residual = after(residual, *gathers[0].second)
    mid_scale = rms_scale(residual)
    mid_hat = residual * mid_scale
    mid = group_gather((mid_hat * ffn_gain_r).astype(bf16))
    mid_t = [turn(a, model) for a in mid]

    out_parts, mid_parts, sums = [], [], []

    def step_all(*which):
        return [a for i in which for a in sums[i].advance()]

    for k in range(chunks):
        waits = []
        if k == 0:
            waits = gathers[1].second
        elif k == 1:
            waits = gathers[2].second
        else:
            waits = step_all(0)
        if k:
            waits = waits + [mid_parts[-1][0]]
        parts = ffn_call(
            tile,
            CHUNKS[k],
            [after(mid[0], *waits), *mid[1:]],
            mid_t,
            cot,
            cot_t,
            gathers[k].blocks(),
        )
        out_parts.append(parts[:members])
        mid_parts.append(parts[members : 2 * members])
        sums.append(Reduction(parts[2 * members :]))

    d_mid = group_scatter(mid_parts)
    ffn_gain_part = jnp.sum(d_mid * mid_hat, axis=0)
    d_resid = cot_own.astype(f32) + norm_back(d_mid, mid_hat, mid_scale, ffn_gain_r)
    d_attn = group_gather(d_resid.astype(bf16))
    waits = step_all(0, 1) + step_all(0, 1)
    d_mixed = [dot(d, out_w).astype(bf16) for d in d_attn]
    d_attn_t = [turn(d, model) for d in d_attn]

    calls = 2 if heads % 4 == 0 else 1
    d_in_parts, gain_parts = [], []
    for call in range(calls):
        waits = waits + step_all(2) if call == 0 else step_all(0, 1, 2) + step_all(2)
        parts = attention_back_call(
            after(flip, *waits),
            size,
            call * (heads // calls),
            heads // calls,
            x,
            x_t,
            d_attn_t,
            mixed,
            cosines,
            sines,
            q_gain2,
            k_gain2,
            d_mixed,
            attn_blocks,
        )
        d_in_parts.append(parts[:members])
        gain_parts.append(parts[members])
        sums.append(Reduction(parts[members + 1 :]))
    head_gains = sum(gain_parts)
    waits = step_all(1, 2)
    out_parts[0] = [after(out_parts[0][0], d_in_parts[0][0]), *out_parts[0][1:]]
    d_in = group_scatter(d_in_parts)
    attn_gain_part = jnp.sum(d_in * in_hat, axis=0)
    input_grad = d_resid + norm_back(d_in, in_hat, in_scale, attn_gain_r)
    input_grad = input_grad.astype(bf16).reshape(quarters, size, model)
    if square():
        sums[-1].state[2] = after(sums[-1].state[2], input_grad, *waits)
    input_grad = from_sequence(input_grad)
    while any(r.step < 5 for r in sums):
        step_all(*[i for i, r in enumerate(sums) if r.step < 5])
    ffn_sums = [r.state for r in sums[:chunks]]
    heads_sums = [r.state for r in sums[chunks:]]

    output = (residual + group_scatter(out_parts)).astype(bf16)
    output = from_sequence(output.reshape(quarters, size, model))

    gain_sums = sum_all(
        jnp.concatenate(
            [
                relative(attn_gain_part),
                relative(ffn_gain_part),
                head_gains[0, :64] + head_gains[0, 64:],
                head_gains[1, :64],
            ]
        ),
        ffn_sums[-1][0],
    )

    if members == 2:
        ffn_grads = finish_ffn_call(ffn_sums)
        mine, other = heads_sums[-1]
        heads_sums[-1] = (after(mine, ffn_grads[0]), other)
        q_grad, k_grad, v_grad, out_grad = finish_heads_call(heads_sums)
    else:
        heads_all = [every_member(h) for h in heads_sums]
        every = jnp.concatenate([h[i] for i in range(members) for h in heads_all], axis=0)
        every = every.transpose(1, 0, 2).astype(f32)
        ffn_sums = [every_member(s) for s in ffn_sums]
        q_grad = every[:, :, :128].reshape(rows_here, q_cols)
        k_grad = every[:, :, 128:192].reshape(rows_here, kv_cols)
        v_grad = every[:, :, 192:256].reshape(rows_here, kv_cols)
        out_grad = every[:, :, 256:].reshape(rows_here, q_cols)
        ffn_grads = [
            jnp.concatenate(
                [ffn_sums[k][i][w] for i in range(members) for k in range(chunks)], axis=1
            ).astype(f32)
            for w in range(3)
        ]
    return (
        output,
        input_grad,
        q_grad,
        k_grad,
        v_grad,
        out_grad,
        ffn_grads[0],
        ffn_grads[1],
        ffn_grads[2],
        gain_sums[:model],
        gain_sums[model : 2 * model],
        gain_sums[2 * model : 2 * model + 64],
        gain_sums[2 * model + 64 :],
    )


def solution(mesh):
    dp, seq = mesh.devices.shape
    lines = 4
    fine = Mesh(mesh.devices.reshape(dp // 4, 2, 2, lines, seq // lines), EVERY)
    rows, cols = ("o", "x", "c"), ("z", "s")
    tokens = P(rows, cols, None)
    weight = P(rows, None)
    return jax.shard_map(
        local,
        mesh=fine,
        in_specs=(tokens, P(rows, cols), tokens) + (weight,) * 7 + (P(),) * 4,
        out_specs=(tokens, tokens) + (weight,) * 7 + (P(),) * 4,
        check_vma=False,
    )
```
